32 devices in a mesh: front: 2 (over core), row: 4 (over y, x), col: 4 (over z).
Axes of the slice: x: 2, y: 2, z: 4, core: 2. Of those that a mesh axis runs over, the one named last changes fastest.
Arguments:
- front_matrix: bfloat16 [2, 6, 4, 256, 6, 4, 256], P('front', None, 'row', None, None, 'col'), as said below
- contributions: bfloat16 [2, 4, 4, 32, 256, 256], P('front', 'row', 'col'), may hold values from -3 to 3
- target_front: int32 [2, 4, 4, 32], P('front', 'row', 'col'), may hold values from 0 to 1, as said below
- target_row: int32 [2, 4, 4, 32], P('front', 'row', 'col'), may hold values from 4 to 23, as said below
- target_col: int32 [2, 4, 4, 32], P('front', 'row', 'col'), may hold values from 0 to 22, as said below
- live_count: int32 [2, 4, 4], P('front', 'row', 'col'), may hold values from 24 to 32
Outputs:
- factor: float32 [2, 6, 4, 256, 6, 4, 256], P('front', None, 'row', None, None, 'col')
The draws below stay inside these ranges and needn't reach their ends.
Inputs may be any that keep to these rules, and one draw needn't show every extreme that they name: `front_matrix`: Symmetric; its leading 2 * 2 * 256 rows and columns form a strictly diagonally dominant block with a positive diagonal. `target_front`: among one device's live slots at most 4 aim at one pair of parent front and target_row modulo the number of row devices, and on every device one such pair takes exactly 4. `target_row`: never one of the first 4 tile rows, nor one of the first tile rows as many as the col devices. `target_col`: below the slot's target_row, and congruent to the holding device's col index modulo the number of col devices.
All inputs are finite; a program needn't handle non-finite values.
Results may differ from the reference program's by a relative error of at most 0.0003.
Values may be sent and summed in bfloat16 or wider, within the bound.
A program may use at most 128 MiB of HBM per device.

```python
import jax
import jax.numpy as jnp
from jax import lax

F = 6144
TS = 256
PANEL_TILES = 2
PANELS = 2
SLOTS = 32
FRONTS = 2
NT = 24
RT = 6
CT = 6
CAP = 4
N_ROW = 4
N_COL = 4


def draw_front_matrix(key, part):
    lead_size = 2 * PANEL_TILES * TS
    key_raw, key_lead, key_rest = jax.random.split(jax.random.fold_in(key, 3), 3)
    raw = jax.random.uniform(key_raw, (FRONTS, F, F), jnp.float32, -1.0, 1.0)
    diag_lead = jax.random.uniform(key_lead, (FRONTS, F), jnp.float32, 16.0, 32.0)
    diag_rest = jax.random.uniform(key_rest, (FRONTS, F), jnp.float32, 4.0, 12.0)
    mirrored = 0.5 * (raw + jnp.swapaxes(raw, 1, 2))
    positions = jnp.arange(F)
    in_lead = positions < lead_size
    both_lead = in_lead[:, None] & in_lead[None, :]
    offdiag = jnp.where(both_lead[None], mirrored * (0.9 * 16.0 / lead_size), mirrored)
    diagonal = jnp.where(in_lead[None, :], diag_lead, diag_rest)
    identity = positions[:, None] == positions[None, :]
    matrix = jnp.where(identity[None], diagonal[:, :, None], offdiag)
    return matrix.reshape(FRONTS, RT, N_ROW, TS, CT, N_COL, TS).astype(jnp.bfloat16)


def route_draw(key):
    base_key = jax.random.fold_in(key, 11)
    key_hot, key_order, key_row, key_col = jax.random.split(base_key, 4)
    grid = (FRONTS, N_ROW, N_COL)
    others = FRONTS * N_ROW
    spread = max(others - 1, 1)
    hottest = jax.random.randint(key_hot, grid + (1,), 0, others)
    scores = jax.random.randint(key_order, grid + (spread,), 0, 1 << 20) * spread + jnp.arange(spread)
    ordering = jnp.argsort(scores, axis=-1)
    slot_ids = jnp.arange(SLOTS)
    cycle = jnp.maximum(slot_ids - CAP, 0) % spread
    picked = jnp.take(ordering, cycle, axis=-1)
    destination = jnp.where(slot_ids < CAP, hottest, (hottest + 1 + picked) % others)
    own_front = jnp.arange(FRONTS).reshape(FRONTS, 1, 1, 1)
    fronts_to = (own_front + destination // N_ROW) % FRONTS
    row_class = destination % N_ROW
    lowest = max(2 * PANEL_TILES, N_COL)
    smallest = (lowest - row_class + N_ROW - 1) // N_ROW
    local_row = jax.random.randint(key_row, grid + (SLOTS,), smallest, RT)
    rows_to = local_row * N_ROW + row_class
    column_class = jnp.arange(N_COL).reshape(1, 1, N_COL, 1)
    largest = (rows_to - column_class + N_COL - 1) // N_COL
    local_col = jax.random.randint(key_col, grid + (SLOTS,), 0, largest)
    cols_to = local_col * N_COL + column_class
    return (fronts_to.astype(jnp.int32), rows_to.astype(jnp.int32), cols_to.astype(jnp.int32))


def draw_target_front(key, part):
    return route_draw(key)[0]


def draw_target_row(key, part):
    return route_draw(key)[1]


def draw_target_col(key, part):
    return route_draw(key)[2]


def place_ends(array, stream_key, low, top_value):
    shape = array.shape
    spot = [jax.random.randint(jax.random.fold_in(stream_key, axis), (), 0, shape[axis]) for axis in range(len(shape))]
    array = array.at[tuple(spot)].set(low)
    longest = shape.index(max(shape))
    spot[longest] = (spot[longest] + 1) % shape[longest]
    return array.at[tuple(spot)].set(top_value)


def block_scale(own_key, extent, shards, low, top_value):
    gain = 1.0
    for dim, shards_of in shards:
        heights = jax.random.uniform(jax.random.fold_in(jax.random.fold_in(own_key, 6), dim), (shards_of,), jnp.float32, low / len(shards), top_value / len(shards))
        gain = gain * jnp.repeat(jnp.exp(heights), extent[dim] // shards_of).reshape((-1,) + (1,) * (len(extent) - 1 - dim))
    return gain


def normal_values(key, dims, width, bound, shards=(), kind=jnp.bfloat16):
    gain = block_scale(key, dims, shards, -0.22, 0.18) if shards else 1.0
    result = jax.random.normal(key, dims, jnp.float32) * width * gain
    return jnp.minimum(jnp.maximum(result, -bound), bound).astype(kind)


def setup_inputs(seed: int = 0) -> dict:
    seeds = jax.random.split(jax.random.key(seed), 7)
    return {
        "front_matrix": draw_front_matrix(jax.random.fold_in(seeds[6], 71), 0),
        "contributions": normal_values(seeds[1], (FRONTS, N_ROW, N_COL, SLOTS, TS, TS), 0.5, 3.0, ((0, 2), (1, 4), (2, 4))),
        "target_front": draw_target_front(jax.random.fold_in(seeds[6], 71), 0),
        "target_row": draw_target_row(jax.random.fold_in(seeds[6], 71), 0),
        "target_col": draw_target_col(jax.random.fold_in(seeds[6], 71), 0),
        "live_count": place_ends(jax.random.randint(seeds[5], (FRONTS, N_ROW, N_COL), 3 * SLOTS // 4, SLOTS + 1), jax.random.fold_in(seeds[5], 1), 3 * SLOTS // 4, SLOTS).astype(jnp.int32),
    }


def mirror_tiles(square, tile_size):
    tile_ids = jnp.arange(square.shape[0]) // tile_size
    return jnp.where(tile_ids[:, None] >= tile_ids[None, :], square, square.T)

def panel_factor(square, tile_size):
    return jnp.linalg.cholesky(mirror_tiles(square, tile_size))

def below_solve(lead_factor, row_block):
    return lax.linalg.triangular_solve(lead_factor, row_block, left_side=False, lower=True, transpose_a=True)

def reference(front_matrix, contributions, target_front, target_row, target_col, live_count):
    sources = FRONTS * N_ROW * N_COL
    contrib_tiles = contributions.reshape(sources, SLOTS, TS, TS)
    fronts_to = target_front.reshape(sources, SLOTS)
    flat_tile = (target_row * NT + target_col).reshape(sources, SLOTS)
    live_slots = (jnp.arange(SLOTS, dtype=jnp.int32)[None, None, None, :] < live_count[..., None]).reshape(sources, SLOTS)
    panel_width = PANEL_TILES * TS

    def one_front(front_number):
        matrix = front_matrix[front_number].astype(jnp.float32).reshape(F, F)
        pieces = matrix.reshape(NT, TS, NT, TS).transpose(0, 2, 1, 3).reshape(NT * NT, TS, TS)
        pieces = jnp.concatenate([pieces, jnp.zeros((1, TS, TS), jnp.float32)], axis=0)

        def add_source(source, totals):
            arrives = live_slots[source] & (fronts_to[source] == front_number)
            where_to = jnp.where(arrives, flat_tile[source], NT * NT).astype(jnp.int32)
            return totals.at[where_to].add(contrib_tiles[source].astype(jnp.float32))
        pieces = lax.fori_loop(0, sources, add_source, pieces)
        matrix = pieces[:NT * NT].reshape(NT, NT, TS, TS).transpose(0, 2, 1, 3).reshape(F, F)
        for panel_number in range(PANELS):
            first_row = panel_number * panel_width
            after_row = first_row + panel_width
            lead_factor = panel_factor(matrix[first_row:after_row, first_row:after_row], TS)
            solved = below_solve(lead_factor, matrix[after_row:, first_row:after_row])
            product = jnp.dot(solved.astype(jnp.float32), solved.T.astype(jnp.float32), precision=lax.Precision.HIGHEST, preferred_element_type=jnp.float32)
            matrix = matrix.at[after_row:, after_row:].set(matrix[after_row:, after_row:] - product)
            column = jnp.concatenate([jnp.zeros((first_row, panel_width), jnp.float32), lead_factor, solved], axis=0)
            matrix = matrix.at[:, first_row:after_row].set(column)
        tile_ids = jnp.arange(F) // TS
        matrix = jnp.where(tile_ids[:, None] >= tile_ids[None, :], matrix, 0.0)
        return matrix.reshape(RT, N_ROW, TS, CT, N_COL, TS)
    return lax.map(one_front, jnp.arange(FRONTS, dtype=jnp.int32))
```

```python
import functools

import jax
import jax.numpy as jnp
from jax import lax
from jax.experimental import pallas as pl
from jax.experimental.pallas import tpu as pltpu
from jax.sharding import PartitionSpec as P

PANEL_TILES = 2
PANELS = 2
LEAD = PANEL_TILES * PANELS
BLOCK = 128
HIGHEST = lax.Precision.HIGHEST
NT = (((1,), (1,)), ((), ()))
F32 = jnp.float32
BF16 = jnp.bfloat16


def mm(a, b):
    return jnp.dot(a, b, precision=HIGHEST, preferred_element_type=F32)


def mm_nt(a, b):
    return lax.dot_general(a, b, NT, precision=HIGHEST, preferred_element_type=F32)


def split(x):
    hi = x.astype(BF16)
    return hi, (x - hi.astype(F32)).astype(BF16)


def mm3_nt(a, b):
    (ah, al), (bh, bl) = a, b
    one = functools.partial(lax.dot_general, dimension_numbers=NT, preferred_element_type=F32)
    return one(ah, bh) + (one(ah, bl) + one(al, bh))


def eliminate(block):
    groups = BLOCK // 8
    upper = [block[8 * i : 8 * i + 8, :] for i in range(groups)]
    rows = lax.broadcasted_iota(jnp.int32, (8, BLOCK), 0)
    lanes = lax.broadcasted_iota(jnp.int32, (8, BLOCK), 1)
    inverse = [jnp.where(rows + 8 * i == lanes, 1.0, 0.0).astype(F32) for i in range(groups)]
    sub = lax.broadcasted_iota(jnp.int32, (8, 1), 0)
    for j in range(BLOCK):
        g, s = divmod(j, 8)
        row_u = upper[g][s : s + 1, :]
        row_i = inverse[g][s : s + 1, :]
        scale = 1.0 / row_u[:, j : j + 1]
        row_u = row_u * scale
        row_i = row_i * scale
        for i in range(g, groups):
            column = upper[i][:, j : j + 1]
            if i == g:
                if s == 7:
                    continue
                column = jnp.where(sub > s, column, 0.0)
            upper[i] = upper[i] - column * row_u
            inverse[i] = inverse[i] - column * row_i
    return jnp.concatenate(upper, axis=0), jnp.concatenate(inverse, axis=0)


def factor_panel(work, lower, inverse, base):
    size = work.shape[0]
    ids = lax.broadcasted_iota(jnp.int32, (size, size), 0)
    inverse[...] = jnp.where(
        ids == lax.broadcasted_iota(jnp.int32, (size, size), 1), 1.0, 0.0
    ).astype(F32)
    row_ids = lax.broadcasted_iota(jnp.int32, (size, BLOCK), 0)
    eye = lax.broadcasted_iota(jnp.int32, (BLOCK, BLOCK), 0) == lax.broadcasted_iota(
        jnp.int32, (BLOCK, BLOCK), 1
    )
    above = lax.broadcasted_iota(jnp.int32, (BLOCK, BLOCK), 0) <= lax.broadcasted_iota(
        jnp.int32, (BLOCK, BLOCK), 1
    )

    def step(k, carry):
        start = pl.multiple_of(k * BLOCK, BLOCK)
        here = pl.ds(start, BLOCK)
        upper, unit = eliminate(work[here, here])
        diagonal = jnp.sum(jnp.where(eye, upper, 0.0), axis=1, keepdims=True)
        root = lax.rsqrt(diagonal)
        root = root * (1.5 - 0.5 * diagonal * root * root)
        small = unit * root
        column = mm_nt(work[:, here], small)
        below = jnp.where(row_ids >= start + BLOCK, column, 0.0)
        lower[pl.ds(base, size), pl.ds(pl.multiple_of(base + start, BLOCK), BLOCK)] = below
        lower[
            pl.ds(pl.multiple_of(base + start, BLOCK), BLOCK),
            pl.ds(pl.multiple_of(base + start, BLOCK), BLOCK),
        ] = jnp.where(above, upper * root, 0.0).T
        solved = mm(small, inverse[here, :])
        inverse[here, :] = solved
        work[...] -= mm_nt(below, below)
        inverse[...] -= mm(below, solved)
        return carry

    lax.fori_loop(0, size // BLOCK, step, 0)


def load_square(lead, work, row0, col0, tile):
    for i in range(PANEL_TILES):
        for j in range(PANEL_TILES):
            work[i * tile : (i + 1) * tile, j * tile : (j + 1) * tile] = lead[
                row0 + i, col0 + j
            ].astype(F32)


def first_kernel(tile, lead, lower, inverse, work):
    load_square(lead, work, 0, 0, tile)
    factor_panel(work, lower, inverse, 0)


def second_kernel(tile, n_row, n_col, spot, lead, lower0, inverse0, high, low, own, work, lower, inverse):
    width = PANEL_TILES * tile
    load_square(lead, work, PANEL_TILES, 0, tile)
    left = mm_nt(work[...], inverse0[...])
    load_square(lead, work, PANEL_TILES, PANEL_TILES, tile)
    work[...] -= mm_nt(left, left)
    lower[:width, :width] = lower0[...]
    lower[:width, width:] = jnp.zeros((width, width), F32)
    lower[width:, :width] = left
    factor_panel(work, lower, inverse, width)
    corner = -mm(inverse[...], mm(left, inverse0[...]))
    for r, c, value in (
        (0, 0, inverse0[...]),
        (0, 1, jnp.zeros((width, width), F32)),
        (1, 0, corner),
        (1, 1, inverse[...]),
    ):
        hi, lo = split(value)
        high[r * width : (r + 1) * width, c * width : (c + 1) * width] = hi
        low[r * width : (r + 1) * width, c * width : (c + 1) * width] = lo
    own[...] = lower[
        pl.ds(pl.multiple_of(jnp.minimum(spot[0], LEAD - 1) * tile, tile), tile),
        pl.ds(pl.multiple_of(jnp.minimum(spot[1], LEAD - 1) * tile, tile), tile),
    ]


def whole(space=pltpu.VMEM):
    return pl.BlockSpec(memory_space=space)


def estimate(us, size):
    return pl.CostEstimate(flops=int(us * 1e9), bytes_accessed=size, transcendentals=0)


def lead_factor(lead, spot, tile, n_row, n_col):
    width = PANEL_TILES * tile
    square = jax.ShapeDtypeStruct((width, width), F32)
    params = pltpu.CompilerParams(vmem_limit_bytes=48 << 20)
    lower0, inverse0 = pl.pallas_call(
        functools.partial(first_kernel, tile),
        out_shape=(square, square),
        in_specs=[whole()],
        out_specs=(whole(), whole()),
        scratch_shapes=[pltpu.VMEM((width, width), F32)],
        compiler_params=params,
        cost_estimate=estimate(60, 1 << 20),
        name="lead_first",
    )(lead)
    full = (2 * width, 2 * width)
    high, low, own = pl.pallas_call(
        functools.partial(second_kernel, tile, n_row, n_col),
        out_shape=(
            jax.ShapeDtypeStruct(full, BF16),
            jax.ShapeDtypeStruct(full, BF16),
            jax.ShapeDtypeStruct((tile, tile), F32),
        ),
        in_specs=[whole(pltpu.SMEM)] + [whole()] * 3,
        out_specs=(whole(),) * 3,
        scratch_shapes=[
            pltpu.VMEM((width, width), F32),
            pltpu.VMEM(full, F32),
            pltpu.VMEM((width, width), F32),
        ],
        compiler_params=params,
        cost_estimate=estimate(60, 1 << 20),
        name="lead_second",
    )(spot, lead, lower0, inverse0)
    return high, low, own


def pack_kernel(count, capacity, source, tiles, *rest):
    buckets, sems = rest[:count], rest[count]
    copies = []
    for k in range(count):
        for p in range(capacity):
            n = k * capacity + p
            copies.append(
                pltpu.make_async_copy(tiles.at[source[n]], buckets[k].at[p], sems.at[n])
            )
    for copy in copies:
        copy.start()
    for copy in copies:
        copy.wait()


def route_tiles(contributions, target_front, target_row, target_col, live_count, tile_cols, n_front, n_row, n_col):
    slots = contributions.shape[3]
    tile = contributions.shape[4]
    tiles = contributions.reshape(slots, tile, tile)
    fronts_to = target_front.reshape(slots)
    rows_to = target_row.reshape(slots)
    cols_to = target_col.reshape(slots)
    ids = jnp.arange(slots, dtype=jnp.int32)
    live = ids < live_count.reshape(())
    count = n_front * n_row
    capacity = max(2, -(-slots // count))
    me = lax.axis_index("front") * n_row + lax.axis_index("row")
    local_tile = rows_to // n_row * tile_cols + cols_to // n_col
    bucket_of = jnp.bitwise_xor(fronts_to * n_row + rows_to % n_row, me)
    earlier = (bucket_of[:, None] == bucket_of[None, :]) & live[None, :] & (ids[None, :] < ids[:, None])
    place = bucket_of * capacity + jnp.sum(earlier.astype(jnp.int32), axis=1)
    matches = (place[None, :] == jnp.arange(count * capacity, dtype=jnp.int32)[:, None]) & live[None, :]
    source = jnp.sum(jnp.where(matches, ids[None, :], 0), axis=1)
    filled = jnp.any(matches, axis=1)
    targets = jnp.sum(jnp.where(matches, local_tile[None, :], 0), axis=1)
    targets = jnp.where(filled, targets, -1)
    buckets = pl.pallas_call(
        functools.partial(pack_kernel, count, capacity),
        out_shape=tuple(jax.ShapeDtypeStruct((capacity, tile, tile), BF16) for _ in range(count)),
        in_specs=[whole(pltpu.SMEM), whole(pl.ANY)],
        out_specs=tuple(whole(pl.ANY) for _ in range(count)),
        scratch_shapes=[pltpu.SemaphoreType.DMA((count * capacity,))],
        name="pack",
    )(source, tiles)
    axes = ("front", "row")
    received = [buckets[0]]
    for k in range(1, count):
        received.append(lax.ppermute(buckets[k], axes, [(i, i ^ k) for i in range(count)]))
    everyone = lax.all_gather(targets.reshape(count, capacity), axes)
    everyone = everyone.reshape(count, count, capacity)
    arrived = jnp.stack(
        [everyone[jnp.bitwise_xor(me, k), k] for k in range(count)]
    ).reshape(-1)
    return received, arrived


def extend_kernel(count, capacity, tile_cols, tile, arrived, front, *rest):
    received, out = rest[:count], rest[count]
    row = pl.program_id(0)
    out[...] = front[...].astype(F32)
    for k in range(count):
        for p in range(capacity):
            target = arrived[k * capacity + p]

            @pl.when((target >= 0) & (target // tile_cols == row))
            def _():
                column = pl.multiple_of(target % tile_cols * tile, tile)
                out[:, pl.ds(column, tile)] += received[k][p].astype(F32)


def extend(front, received, arrived, tile_rows, tile_cols, tile):
    count, capacity = len(received), received[0].shape[0]
    rows, cols = front.shape
    return pl.pallas_call(
        functools.partial(extend_kernel, count, capacity, tile_cols, tile),
        out_shape=jax.ShapeDtypeStruct((rows, cols), F32),
        grid=(tile_rows,),
        in_specs=[whole(pltpu.SMEM), pl.BlockSpec((tile, cols), lambda a: (a, 0))] + [whole()] * count,
        out_specs=pl.BlockSpec((tile, cols), lambda a: (a, 0)),
        compiler_params=pltpu.CompilerParams(vmem_limit_bytes=48 << 20),
        cost_estimate=estimate(8, rows * cols * 6),
        name="extend",
    )(arrived, front, *received)


def solve_rows(gathered, start, high, low, tile):
    parts = [split(gathered[c, pl.ds(start, tile), :]) for c in range(LEAD)]
    solved = []
    for n in range(LEAD):
        total = None
        for c in range(n + 1):
            rows = slice(n * tile, (n + 1) * tile)
            cols = slice(c * tile, (c + 1) * tile)
            term = mm3_nt(parts[c], (high[rows, cols], low[rows, cols]))
            total = term if total is None else total + term
        solved.append(total)
    return solved


def trailing_kernel(
    tile, n_row, n_col, tile_cols, row0, col0, spot, work, by_row, by_col, high, low, own, out, cols_hi, cols_lo, rows_f
):
    a = pl.program_id(0)
    row_index, col_index = spot[0], spot[1]

    @pl.when(a == 0)
    def _():
        def body(b, carry):
            start = pl.multiple_of(b * tile, tile)
            solved = solve_rows(by_col, start, high, low, tile)
            for n in range(LEAD):
                hi, lo = split(solved[n])
                cols_hi[pl.ds(start, tile), n * tile : (n + 1) * tile] = hi
                cols_lo[pl.ds(start, tile), n * tile : (n + 1) * tile] = lo
            return carry

        lax.fori_loop(0, tile_cols - col0, body, 0)

    global_row = a * n_row + row_index
    below = global_row >= LEAD

    def finish(b, value):
        out[:, b * tile : (b + 1) * tile] = value

    @pl.when(below)
    def _():
        start = pl.multiple_of((a - row0) * tile, tile)
        solved = solve_rows(by_row, start, high, low, tile)
        for n in range(LEAD):
            rows_f[n] = solved[n]
        rows = split(jnp.concatenate(solved, axis=1))
        for b in range(tile_cols):
            global_col = b * n_col + col_index
            if b * n_col < LEAD:

                @pl.when(global_col < LEAD)
                def _():
                    finish(b, rows_f[jnp.minimum(global_col, LEAD - 1)])

            if b * n_col + n_col > LEAD:

                @pl.when((global_col >= LEAD) & (global_col <= global_row))
                def _():
                    at = slice((b - col0) * tile, (b - col0 + 1) * tile)
                    update = mm3_nt(rows, (cols_hi[at, :], cols_lo[at, :]))
                    finish(b, work[:, b * tile : (b + 1) * tile] - update)

                @pl.when((global_col >= LEAD) & (global_col > global_row))
                def _():
                    finish(b, jnp.zeros((tile, tile), F32))

    @pl.when(jnp.logical_not(below))
    def _():
        for b in range(tile_cols):
            finish(b, jnp.zeros((tile, tile), F32))

        @pl.when((col_index < LEAD) & (col_index <= row_index))
        def _():
            finish(0, own[...])


def trailing(work, by_row, by_col, high, low, own, spot, tile, n_row, n_col, tile_rows, tile_cols, row0, col0):
    rows, cols = work.shape
    width = LEAD * tile
    count = (tile_cols - col0) * tile
    return pl.pallas_call(
        functools.partial(trailing_kernel, tile, n_row, n_col, tile_cols, row0, col0),
        out_shape=jax.ShapeDtypeStruct((rows, cols), F32),
        grid=(tile_rows,),
        in_specs=[whole(pltpu.SMEM), pl.BlockSpec((tile, cols), lambda a: (a, 0))] + [whole()] * 5,
        out_specs=pl.BlockSpec((tile, cols), lambda a: (a, 0)),
        scratch_shapes=[
            pltpu.VMEM((count, width), BF16),
            pltpu.VMEM((count, width), BF16),
            pltpu.VMEM((LEAD, tile, tile), F32),
        ],
        compiler_params=pltpu.CompilerParams(vmem_limit_bytes=56 << 20),
        cost_estimate=estimate(25, rows * cols * 8),
        name="trailing",
    )(spot, work, by_row, by_col, high, low, own)


def per_device(front_matrix, contributions, target_front, target_row, target_col, live_count):
    tile_rows = front_matrix.shape[1]
    tile = front_matrix.shape[3]
    tile_cols = front_matrix.shape[4]
    n_front = lax.axis_size("front")
    n_row = lax.axis_size("row")
    n_col = lax.axis_size("col")
    spot = jnp.stack([lax.axis_index("row"), lax.axis_index("col")]).astype(jnp.int32)
    front = front_matrix.reshape(tile_rows * tile, tile_cols * tile)
    row0, col0 = LEAD // n_row, LEAD // n_col

    lead = lax.all_gather(front[:tile, :tile], ("row", "col"))
    lead = lead.reshape(n_row, n_col, tile, tile)[:LEAD, :LEAD]
    received, arrived = route_tiles(
        contributions, target_front, target_row, target_col, live_count, tile_cols, n_front, n_row, n_col
    )
    high, low, own = lead_factor(lead, spot, tile, n_row, n_col)
    work = extend(front, received, arrived, tile_rows, tile_cols, tile)
    piece = work[row0 * tile :, :tile]
    by_row = lax.all_gather(piece, "col")[:LEAD]
    mirrored = lax.ppermute(
        piece,
        ("row", "col"),
        [(r * n_col + c, c * n_col + r) for r in range(n_row) for c in range(n_col)],
    )
    by_col = lax.all_gather(mirrored, "row")[:LEAD]
    factor = trailing(
        work, by_row, by_col, high, low, own, spot, tile, n_row, n_col, tile_rows, tile_cols, row0, col0
    )
    return factor.reshape(1, tile_rows, 1, tile, tile_cols, 1, tile)


def solution(mesh):
    in_specs = (
        P("front", None, "row", None, None, "col", None),
        P("front", "row", "col", None, None, None),
        P("front", "row", "col", None),
        P("front", "row", "col", None),
        P("front", "row", "col", None),
        P("front", "row", "col"),
    )
    out_specs = P("front", None, "row", None, None, "col", None)
    return jax.shard_map(
        per_device, mesh=mesh, in_specs=in_specs, out_specs=out_specs, check_vma=False
    )
```

```python
import functools

import jax
import jax.numpy as jnp
from jax import lax
from jax.experimental import pallas as pl
from jax.experimental.pallas import tpu as pltpu
from jax.sharding import PartitionSpec as P

PANEL_TILES = 2
PANELS = 2
LEAD = PANEL_TILES * PANELS
BLOCK = 128
LANES = 128
TOP = 32000.0
HIGHEST = lax.Precision.HIGHEST
NT = (((1,), (1,)), ((), ()))
F32 = jnp.float32
BF16 = jnp.bfloat16


def mm(a, b):
    return jnp.dot(a, b, precision=HIGHEST, preferred_element_type=F32)


def mm_nt(a, b):
    return lax.dot_general(a, b, NT, precision=HIGHEST, preferred_element_type=F32)


def split(x):
    hi = x.astype(BF16)
    return hi, (x - hi.astype(F32)).astype(BF16)


def mm3_nt(a, b):
    (ah, al), (bh, bl) = a, b
    one = functools.partial(lax.dot_general, dimension_numbers=NT, preferred_element_type=F32)
    return one(ah, bh) + (one(ah, bl) + one(al, bh))


def eliminate(block):
    groups = BLOCK // 8
    upper = [block[8 * i : 8 * i + 8, :] for i in range(groups)]
    rows = lax.broadcasted_iota(jnp.int32, (8, BLOCK), 0)
    lanes = lax.broadcasted_iota(jnp.int32, (8, BLOCK), 1)
    inverse = [jnp.where(rows + 8 * i == lanes, 1.0, 0.0).astype(F32) for i in range(groups)]
    sub = lax.broadcasted_iota(jnp.int32, (8, 1), 0)
    for j in range(BLOCK):
        g, s = divmod(j, 8)
        row_u = upper[g][s : s + 1, :]
        row_i = inverse[g][s : s + 1, :]
        scale = 1.0 / row_u[:, j : j + 1]
        row_u = row_u * scale
        row_i = row_i * scale
        for i in range(g, groups):
            column = upper[i][:, j : j + 1]
            if i == g:
                if s == 7:
                    continue
                column = jnp.where(sub > s, column, 0.0)
            upper[i] = upper[i] - column * row_u
            inverse[i] = inverse[i] - column * row_i
    return jnp.concatenate(upper, axis=0), jnp.concatenate(inverse, axis=0)


def factor_panel(work, lower, inverse, base):
    size = work.shape[0]
    ids = lax.broadcasted_iota(jnp.int32, (size, size), 0)
    inverse[...] = jnp.where(
        ids == lax.broadcasted_iota(jnp.int32, (size, size), 1), 1.0, 0.0
    ).astype(F32)
    row_ids = lax.broadcasted_iota(jnp.int32, (size, BLOCK), 0)
    eye = lax.broadcasted_iota(jnp.int32, (BLOCK, BLOCK), 0) == lax.broadcasted_iota(
        jnp.int32, (BLOCK, BLOCK), 1
    )
    above = lax.broadcasted_iota(jnp.int32, (BLOCK, BLOCK), 0) <= lax.broadcasted_iota(
        jnp.int32, (BLOCK, BLOCK), 1
    )

    def step(k, carry):
        start = pl.multiple_of(k * BLOCK, BLOCK)
        here = pl.ds(start, BLOCK)
        upper, unit = eliminate(work[here, here])
        diagonal = jnp.sum(jnp.where(eye, upper, 0.0), axis=1, keepdims=True)
        root = lax.rsqrt(diagonal)
        root = root * (1.5 - 0.5 * diagonal * root * root)
        small = unit * root
        column = mm_nt(work[:, here], small)
        below = jnp.where(row_ids >= start + BLOCK, column, 0.0)
        lower[pl.ds(base, size), pl.ds(pl.multiple_of(base + start, BLOCK), BLOCK)] = below
        lower[
            pl.ds(pl.multiple_of(base + start, BLOCK), BLOCK),
            pl.ds(pl.multiple_of(base + start, BLOCK), BLOCK),
        ] = jnp.where(above, upper * root, 0.0).T
        solved = mm(small, inverse[here, :])
        inverse[here, :] = solved
        work[...] -= mm_nt(below, below)
        inverse[...] -= mm(below, solved)
        return carry

    lax.fori_loop(0, size // BLOCK, step, 0)


def load_square(spot, lead, work, row0, col0, tile):
    for k, tiles in enumerate(lead):
        row = jnp.bitwise_xor(spot[0], k) - row0

        @pl.when((row >= 0) & (row < PANEL_TILES))
        def _():
            at = pl.ds(pl.multiple_of(row * tile, tile), tile)
            for j in range(PANEL_TILES):
                place = jnp.bitwise_xor(spot[1], col0 + j)
                work[at, j * tile : (j + 1) * tile] = tiles[place].astype(F32)


def first_kernel(tile, n_row, spot, *rest):
    lead, (lower, inverse, work) = rest[:n_row], rest[n_row:]
    load_square(spot, lead, work, 0, 0, tile)
    factor_panel(work, lower, inverse, 0)


def second_kernel(tile, n_row, spot, *rest):
    lead, (lower0, inverse0, high, low, own, work, lower, inverse) = rest[:n_row], rest[n_row:]
    width = PANEL_TILES * tile
    load_square(spot, lead, work, PANEL_TILES, 0, tile)
    left = mm_nt(work[...], inverse0[...])
    load_square(spot, lead, work, PANEL_TILES, PANEL_TILES, tile)
    work[...] -= mm_nt(left, left)
    lower[:width, :width] = lower0[...]
    lower[:width, width:] = jnp.zeros((width, width), F32)
    lower[width:, :width] = left
    factor_panel(work, lower, inverse, width)
    corner = -mm(inverse[...], mm(left, inverse0[...]))
    for r, c, value in (
        (0, 0, inverse0[...]),
        (0, 1, jnp.zeros((width, width), F32)),
        (1, 0, corner),
        (1, 1, inverse[...]),
    ):
        hi, lo = split(value)
        high[r * width : (r + 1) * width, c * width : (c + 1) * width] = hi
        low[r * width : (r + 1) * width, c * width : (c + 1) * width] = lo
    own[...] = lower[
        pl.ds(pl.multiple_of(jnp.minimum(spot[0], LEAD - 1) * tile, tile), tile),
        pl.ds(pl.multiple_of(jnp.minimum(spot[1], LEAD - 1) * tile, tile), tile),
    ]


def whole(space=pltpu.VMEM):
    return pl.BlockSpec(memory_space=space)


def estimate(us, size):
    return pl.CostEstimate(flops=int(us * 1e9), bytes_accessed=size, transcendentals=0)


def lead_first(lead, spot, tile):
    width = PANEL_TILES * tile
    square = jax.ShapeDtypeStruct((width, width), F32)
    return pl.pallas_call(
        functools.partial(first_kernel, tile, len(lead)),
        out_shape=(square, square),
        in_specs=[whole(pltpu.SMEM)] + [whole()] * len(lead),
        out_specs=(whole(), whole()),
        scratch_shapes=[pltpu.VMEM((width, width), F32)],
        compiler_params=pltpu.CompilerParams(vmem_limit_bytes=48 << 20),
        cost_estimate=estimate(60, 1 << 20),
        name="lead_first",
    )(spot, *lead)


def lead_second(lead, lower0, inverse0, spot, tile):
    width = PANEL_TILES * tile
    full = (2 * width, 2 * width)
    return pl.pallas_call(
        functools.partial(second_kernel, tile, len(lead)),
        out_shape=(
            jax.ShapeDtypeStruct(full, BF16),
            jax.ShapeDtypeStruct(full, BF16),
            jax.ShapeDtypeStruct((tile, tile), F32),
        ),
        in_specs=[whole(pltpu.SMEM)] + [whole()] * (len(lead) + 2),
        out_specs=(whole(),) * 3,
        scratch_shapes=[
            pltpu.VMEM((width, width), F32),
            pltpu.VMEM(full, F32),
            pltpu.VMEM((width, width), F32),
        ],
        compiler_params=pltpu.CompilerParams(vmem_limit_bytes=48 << 20),
        cost_estimate=estimate(60, 1 << 20),
        name="lead_second",
    )(spot, *lead, lower0, inverse0)


def pack_kernel(count, capacity, source, tiles, *rest):
    buckets, (held, in_sems, out_sems) = rest[:count], rest[count:]
    loads, stores = [], []
    for n in range(count * capacity):
        loads.append(pltpu.make_async_copy(tiles.at[source[n]], held.at[n], in_sems.at[n]))
        into = buckets[n // capacity].at[n % capacity]
        stores.append(pltpu.make_async_copy(held.at[n], into, out_sems.at[n]))
    for load in loads:
        load.start()
    for load, store in zip(loads, stores):
        load.wait()
        store.start()
    for store in stores:
        store.wait()


def route_tiles(contributions, target_front, target_row, target_col, live_count, tile_cols, n_front, n_row, n_col):
    slots = contributions.shape[3]
    tile = contributions.shape[4]
    tiles = contributions.reshape(slots, tile, tile)
    fronts_to = target_front.reshape(slots)
    rows_to = target_row.reshape(slots)
    cols_to = target_col.reshape(slots)
    ids = jnp.arange(slots, dtype=jnp.int32)
    live = ids < live_count.reshape(())
    count = n_front * n_row
    capacity = max(2, -(-slots // count))
    me = lax.axis_index("front") * n_row + lax.axis_index("row")
    local_tile = rows_to // n_row * tile_cols + cols_to // n_col
    bucket_of = jnp.bitwise_xor(fronts_to * n_row + rows_to % n_row, me)
    earlier = (bucket_of[:, None] == bucket_of[None, :]) & live[None, :] & (ids[None, :] < ids[:, None])
    place = bucket_of * capacity + jnp.sum(earlier.astype(jnp.int32), axis=1)
    matches = (place[None, :] == jnp.arange(count * capacity, dtype=jnp.int32)[:, None]) & live[None, :]
    source = jnp.sum(jnp.where(matches, ids[None, :], 0), axis=1)
    filled = jnp.any(matches, axis=1)
    targets = jnp.sum(jnp.where(matches, local_tile[None, :], 0), axis=1)
    targets = jnp.where(filled, targets, -1)
    buckets = pl.pallas_call(
        functools.partial(pack_kernel, count, capacity),
        out_shape=tuple(jax.ShapeDtypeStruct((capacity, tile, tile), BF16) for _ in range(count)),
        in_specs=[whole(pltpu.SMEM), whole(pl.ANY)],
        out_specs=tuple(whole(pl.ANY) for _ in range(count)),
        scratch_shapes=[
            pltpu.VMEM((count * capacity, tile, tile), BF16),
            pltpu.SemaphoreType.DMA((count * capacity,)),
            pltpu.SemaphoreType.DMA((count * capacity,)),
        ],
        compiler_params=pltpu.CompilerParams(vmem_limit_bytes=16 << 20),
        cost_estimate=estimate(5, 2 * slots * tile * tile * 2),
        name="pack",
    )(source, tiles)
    axes = ("front", "row")
    received = [buckets[0]]
    for k in range(1, count):
        received.append(lax.ppermute(buckets[k], axes, [(i, i ^ k) for i in range(count)]))
    everyone = lax.all_gather(targets.reshape(count, capacity), axes)
    everyone = everyone.reshape(count, count, capacity)
    arrived = jnp.stack(
        [everyone[jnp.bitwise_xor(me, k), k] for k in range(count)]
    ).reshape(-1)
    return received, arrived


def extend_kernel(count, capacity, tile_cols, tile, arrived, front, *rest):
    received, out = rest[:count], rest[count]
    row = pl.program_id(0)
    out[...] = front[...].astype(F32)
    for k in range(count):
        for p in range(capacity):
            target = arrived[k * capacity + p]

            @pl.when((target >= 0) & (target // tile_cols == row))
            def _():
                column = pl.multiple_of(target % tile_cols * tile, tile)
                out[:, pl.ds(column, tile)] += received[k][p].astype(F32)


def extend(front, received, arrived, tile_rows, tile_cols, tile):
    count, capacity = len(received), received[0].shape[0]
    rows, cols = front.shape
    return pl.pallas_call(
        functools.partial(extend_kernel, count, capacity, tile_cols, tile),
        out_shape=jax.ShapeDtypeStruct((rows, cols), F32),
        grid=(tile_rows,),
        in_specs=[whole(pltpu.SMEM), pl.BlockSpec((tile, cols), lambda a: (a, 0))] + [whole()] * count,
        out_specs=pl.BlockSpec((tile, cols), lambda a: (a, 0)),
        compiler_params=pltpu.CompilerParams(vmem_limit_bytes=48 << 20),
        cost_estimate=estimate(8, rows * cols * 6),
        name="extend",
    )(arrived, front, *received)


def solve_rows(coded, scales, index, t, high, low, tile):
    start = pl.multiple_of(t * tile, tile)
    parts = []
    for c in range(LEAD):
        k = jnp.bitwise_xor(index, c)
        values = coded[k, pl.ds(start, tile), :].astype(jnp.int32).astype(F32)
        parts.append(split(values * scales[k, t]))
    solved = []
    for n in range(LEAD):
        total = None
        for c in range(n + 1):
            rows = slice(n * tile, (n + 1) * tile)
            cols = slice(c * tile, (c + 1) * tile)
            term = mm3_nt(parts[c], (high[rows, cols], low[rows, cols]))
            total = term if total is None else total + term
        solved.append(total)
    return solved


def trailing_kernel(
    tile, n_row, n_col, tile_cols, row0, col0, spot, row_scales, col_scales, work, by_row, by_col, high, low, own, out, cols_hi, cols_lo, rows_f
):
    a = pl.program_id(0)
    row_index, col_index = spot[0], spot[1]
    pieces = tile // LANES

    @pl.when(a == 0)
    def _():
        def body(b, carry):
            start = pl.multiple_of(b * tile, tile)
            solved = solve_rows(by_col, col_scales, row_index, b, high, low, tile)
            for n in range(LEAD):
                hi, lo = split(solved[n])
                cols_hi[pl.ds(start, tile), n * tile : (n + 1) * tile] = hi
                cols_lo[pl.ds(start, tile), n * tile : (n + 1) * tile] = lo
            return carry

        lax.fori_loop(0, tile_cols - col0, body, 0)

    global_row = a * n_row + row_index
    below = global_row >= LEAD

    def finish(b, value):
        for part in range(pieces):
            lanes = value[:, part * LANES : (part + 1) * LANES]
            out[pl.ds(b * pieces + part, tile, stride=tile_cols * pieces), :] = lanes

    @pl.when(below)
    def _():
        solved = solve_rows(by_row, row_scales, col_index, a - row0, high, low, tile)
        for n in range(LEAD):
            rows_f[n] = solved[n]
        rows = split(jnp.concatenate(solved, axis=1))
        for b in range(tile_cols):
            global_col = b * n_col + col_index
            if b * n_col < LEAD:

                @pl.when(global_col < LEAD)
                def _():
                    finish(b, rows_f[jnp.minimum(global_col, LEAD - 1)])

            if b * n_col + n_col > LEAD:

                @pl.when((global_col >= LEAD) & (global_col <= global_row))
                def _():
                    at = slice((b - col0) * tile, (b - col0 + 1) * tile)
                    update = mm3_nt(rows, (cols_hi[at, :], cols_lo[at, :]))
                    finish(b, work[:, b * tile : (b + 1) * tile] - update)

                @pl.when((global_col >= LEAD) & (global_col > global_row))
                def _():
                    finish(b, jnp.zeros((tile, tile), F32))

    @pl.when(jnp.logical_not(below))
    def _():
        for b in range(tile_cols):
            finish(b, jnp.zeros((tile, tile), F32))

        @pl.when((col_index < LEAD) & (col_index <= row_index))
        def _():
            finish(0, own[...])


def trailing(work, by_row, by_col, high, low, own, spot, tile, n_row, n_col, tile_rows, tile_cols, row0, col0):
    rows, cols = work.shape
    width = LEAD * tile
    count = (tile_cols - col0) * tile
    lines = tile * cols // LANES
    return pl.pallas_call(
        functools.partial(trailing_kernel, tile, n_row, n_col, tile_cols, row0, col0),
        out_shape=jax.ShapeDtypeStruct((tile_rows * lines, LANES), F32),
        grid=(tile_rows,),
        in_specs=[whole(pltpu.SMEM)] * 3
        + [pl.BlockSpec((tile, cols), lambda a: (a, 0))]
        + [whole()] * 5,
        out_specs=pl.BlockSpec((lines, LANES), lambda a: (a, 0)),
        scratch_shapes=[
            pltpu.VMEM((count, width), BF16),
            pltpu.VMEM((count, width), BF16),
            pltpu.VMEM((LEAD, tile, tile), F32),
        ],
        compiler_params=pltpu.CompilerParams(vmem_limit_bytes=56 << 20),
        cost_estimate=estimate(25, rows * cols * 8),
        name="trailing",
    )(spot, decode_scales(by_row, tile), decode_scales(by_col, tile), work, by_row, by_col, high, low, own)


def encode(piece, tile):
    tiles = piece.reshape(-1, tile, tile)
    largest = jnp.max(jnp.abs(tiles), axis=(1, 2))
    power = jnp.floor(jnp.log2(jnp.maximum(largest, 1e-30))) + 1.0
    half = jnp.floor(0.5 * power)
    shrunk = tiles * jnp.exp2(-half)[:, None, None]
    codes = jnp.round(shrunk * (jnp.exp2(half - power) * TOP)[:, None, None]).astype(jnp.int16)
    line = jnp.zeros((16, tile), jnp.int16).at[0, : tiles.shape[0]].set(power.astype(jnp.int16))
    return jnp.concatenate([codes.reshape(-1, tile), line], axis=0)


def decode_scales(coded, tile):
    rows = coded.shape[1] - 16
    return jnp.exp2(coded[:, rows, : rows // tile].astype(F32) - 14.0) * (16384.0 / TOP)


def exchange(piece, axis, size):
    return [piece] + [
        lax.ppermute(piece, axis, [(i, i ^ k) for i in range(size)]) for k in range(1, size)
    ]


def per_device(front_matrix, contributions, target_front, target_row, target_col, live_count):
    tile_rows = front_matrix.shape[1]
    tile = front_matrix.shape[3]
    tile_cols = front_matrix.shape[4]
    n_front = lax.axis_size("front")
    n_row = lax.axis_size("row")
    n_col = lax.axis_size("col")
    spot = jnp.stack([lax.axis_index("row"), lax.axis_index("col")]).astype(jnp.int32)
    row0, col0 = LEAD // n_row, LEAD // n_col

    line = jnp.stack(exchange(front_matrix[0, 0, 0, :, 0, 0, :], "col", n_col))
    lead = exchange(line, "row", n_row)
    front = front_matrix.reshape(tile_rows * tile, tile_cols * tile)
    received, arrived = route_tiles(
        contributions, target_front, target_row, target_col, live_count, tile_cols, n_front, n_row, n_col
    )
    lower0, inverse0 = lead_first(lead, spot, tile)
    arrived, lower0 = lax.optimization_barrier((arrived, lower0))
    work = extend(front, received, arrived, tile_rows, tile_cols, tile)
    coded = encode(work[row0 * tile :, :tile], tile)
    by_row = exchange(coded, "col", n_col)
    mirrored = lax.ppermute(
        coded,
        ("row", "col"),
        [(r * n_col + c, c * n_col + r) for r in range(n_row) for c in range(n_col)],
    )
    by_col = exchange(mirrored, "row", n_row)
    high, low, own = lead_second(lead, lower0, inverse0, spot, tile)
    factor = trailing(
        work,
        jnp.stack(by_row),
        jnp.stack(by_col),
        high,
        low,
        own,
        spot,
        tile,
        n_row,
        n_col,
        tile_rows,
        tile_cols,
        row0,
        col0,
    )
    return factor.reshape(1, tile_rows, 1, tile, tile_cols, 1, tile)


def solution(mesh):
    in_specs = (
        P("front", None, "row", None, None, "col", None),
        P("front", "row", "col", None, None, None),
        P("front", "row", "col", None),
        P("front", "row", "col", None),
        P("front", "row", "col", None),
        P("front", "row", "col"),
    )
    out_specs = P("front", None, "row", None, None, "col", None)
    return jax.shard_map(
        per_device, mesh=mesh, in_specs=in_specs, out_specs=out_specs, check_vma=False
    )
```

```python
import functools

import jax
import jax.numpy as jnp
from jax import lax
from jax.experimental import pallas as pl
from jax.experimental.pallas import tpu as pltpu
from jax.sharding import PartitionSpec as P

PANEL_TILES = 2
PANELS = 2
LEAD = PANEL_TILES * PANELS
BLOCK = 128
LANES = 128
TOP = 32000.0
HIGHEST = lax.Precision.HIGHEST
NT = (((1,), (1,)), ((), ()))
F32 = jnp.float32
BF16 = jnp.bfloat16


def mm(a, b):
    return jnp.dot(a, b, precision=HIGHEST, preferred_element_type=F32)


def mm_nt(a, b):
    return lax.dot_general(a, b, NT, precision=HIGHEST, preferred_element_type=F32)


def split(x):
    hi = x.astype(BF16)
    return hi, (x - hi.astype(F32)).astype(BF16)


def mm3_nt(a, b):
    (ah, al), (bh, bl) = a, b
    one = functools.partial(lax.dot_general, dimension_numbers=NT, preferred_element_type=F32)
    return one(ah, bh) + (one(ah, bl) + one(al, bh))


def eliminate(block):
    groups = BLOCK // 8
    upper = [block[8 * i : 8 * i + 8, :] for i in range(groups)]
    rows = lax.broadcasted_iota(jnp.int32, (8, BLOCK), 0)
    lanes = lax.broadcasted_iota(jnp.int32, (8, BLOCK), 1)
    inverse = [jnp.where(rows + 8 * i == lanes, 1.0, 0.0).astype(F32) for i in range(groups)]
    sub = lax.broadcasted_iota(jnp.int32, (8, 1), 0)
    for j in range(BLOCK):
        g, s = divmod(j, 8)
        row_u = upper[g][s : s + 1, :]
        row_i = inverse[g][s : s + 1, :]
        scale = 1.0 / row_u[:, j : j + 1]
        row_u = row_u * scale
        row_i = row_i * scale
        for i in range(g, groups):
            column = upper[i][:, j : j + 1]
            if i == g:
                if s == 7:
                    continue
                column = jnp.where(sub > s, column, 0.0)
            upper[i] = upper[i] - column * row_u
            inverse[i] = inverse[i] - column * row_i
    return jnp.concatenate(upper, axis=0), jnp.concatenate(inverse, axis=0)


def set_eye(ref):
    ids = lax.broadcasted_iota(jnp.int32, ref.shape, 0)
    ref[...] = jnp.where(ids == lax.broadcasted_iota(jnp.int32, ref.shape, 1), 1.0, 0.0).astype(F32)


def factor_panel(work, lower, inverse, first, last):
    size = work.shape[0]
    row_ids = lax.broadcasted_iota(jnp.int32, (size, BLOCK), 0)
    eye = lax.broadcasted_iota(jnp.int32, (BLOCK, BLOCK), 0) == lax.broadcasted_iota(
        jnp.int32, (BLOCK, BLOCK), 1
    )
    above = lax.broadcasted_iota(jnp.int32, (BLOCK, BLOCK), 0) <= lax.broadcasted_iota(
        jnp.int32, (BLOCK, BLOCK), 1
    )

    def step(k, carry):
        start = pl.multiple_of(k * BLOCK, BLOCK)
        here = pl.ds(start, BLOCK)
        upper, unit = eliminate(work[here, here])
        diagonal = jnp.sum(jnp.where(eye, upper, 0.0), axis=1, keepdims=True)
        root = lax.rsqrt(diagonal)
        root = root * (1.5 - 0.5 * diagonal * root * root)
        small = unit * root
        column = mm_nt(work[:, here], small)
        below = jnp.where(row_ids >= start + BLOCK, column, 0.0)
        lower[:, here] = below
        lower[here, here] = jnp.where(above, upper * root, 0.0).T
        solved = mm(small, inverse[here, :])
        inverse[here, :] = solved
        work[...] -= mm_nt(below, below)
        inverse[...] -= mm(below, solved)
        return carry

    lax.fori_loop(first, last, step, 0)


def load_square(spot, lead, work, row0, col0, tile):
    for k, tiles in enumerate(lead):
        row = jnp.bitwise_xor(spot[0], k) - row0

        @pl.when((row >= 0) & (row < PANEL_TILES))
        def _():
            at = pl.ds(pl.multiple_of(row * tile, tile), tile)
            for j in range(PANEL_TILES):
                place = jnp.bitwise_xor(spot[1], col0 + j)
                work[at, j * tile : (j + 1) * tile] = tiles[place].astype(F32)


def first_kernel(tile, n_row, spot, *rest):
    lead, (lower, inverse, work) = rest[:n_row], rest[n_row:]
    load_square(spot, lead, work, 0, 0, tile)
    set_eye(inverse)
    factor_panel(work, lower, inverse, 0, work.shape[0] // BLOCK)


def second_kernel(tile, n_row, spot, *rest):
    lead, (inverse0, left, work, lower, inverse) = rest[:n_row], rest[n_row:]
    load_square(spot, lead, work, PANEL_TILES, 0, tile)
    left[...] = mm_nt(work[...], inverse0[...])
    load_square(spot, lead, work, PANEL_TILES, PANEL_TILES, tile)
    work[...] -= mm_nt(left[...], left[...])
    set_eye(inverse)
    lower[...] = jnp.zeros_like(lower)
    factor_panel(work, lower, inverse, 0, work.shape[0] // BLOCK // 2)


def third_kernel(tile, spot, lower0, inverse0, left, work1, lower1, inverse1, high, low, own, work, lower, inverse):
    width = PANEL_TILES * tile
    work[...] = work1[...]
    lower[...] = lower1[...]
    inverse[...] = inverse1[...]
    blocks = width // BLOCK
    factor_panel(work, lower, inverse, blocks // 2, blocks)
    corner = -mm(inverse[...], mm(left[...], inverse0[...]))
    for r, c, value in (
        (0, 0, inverse0[...]),
        (0, 1, jnp.zeros((width, width), F32)),
        (1, 0, corner),
        (1, 1, inverse[...]),
    ):
        hi, lo = split(value)
        high[r * width : (r + 1) * width, c * width : (c + 1) * width] = hi
        low[r * width : (r + 1) * width, c * width : (c + 1) * width] = lo
    own[...] = jnp.zeros_like(own)
    for r, c, square in ((0, 0, lower0), (1, 0, left), (1, 1, lower)):
        row, col = spot[0] - r * PANEL_TILES, spot[1] - c * PANEL_TILES

        @pl.when((row >= 0) & (row < PANEL_TILES) & (col >= 0) & (col < PANEL_TILES))
        def _():
            own[...] = square[
                pl.ds(pl.multiple_of(row * tile, tile), tile),
                pl.ds(pl.multiple_of(col * tile, tile), tile),
            ]


def whole(space=pltpu.VMEM):
    return pl.BlockSpec(memory_space=space)


def estimate(us, size):
    return pl.CostEstimate(flops=int(us * 1e9), bytes_accessed=size, transcendentals=0)


def lead_first(lead, spot, tile):
    width = PANEL_TILES * tile
    square = jax.ShapeDtypeStruct((width, width), F32)
    return pl.pallas_call(
        functools.partial(first_kernel, tile, len(lead)),
        out_shape=(square, square),
        in_specs=[whole(pltpu.SMEM)] + [whole()] * len(lead),
        out_specs=(whole(), whole()),
        scratch_shapes=[pltpu.VMEM((width, width), F32)],
        compiler_params=pltpu.CompilerParams(vmem_limit_bytes=48 << 20),
        cost_estimate=estimate(60, 1 << 20),
        name="lead_first",
    )(spot, *lead)


def lead_second(lead, inverse0, spot, tile):
    width = PANEL_TILES * tile
    square = jax.ShapeDtypeStruct((width, width), F32)
    return pl.pallas_call(
        functools.partial(second_kernel, tile, len(lead)),
        out_shape=(square,) * 4,
        in_specs=[whole(pltpu.SMEM)] + [whole()] * (len(lead) + 1),
        out_specs=(whole(),) * 4,
        compiler_params=pltpu.CompilerParams(vmem_limit_bytes=48 << 20),
        cost_estimate=estimate(30, 1 << 20),
        name="lead_second",
    )(spot, *lead, inverse0)


def lead_third(lower0, inverse0, left, work, lower, inverse, spot, tile):
    width = PANEL_TILES * tile
    full = (2 * width, 2 * width)
    return pl.pallas_call(
        functools.partial(third_kernel, tile),
        out_shape=(
            jax.ShapeDtypeStruct(full, BF16),
            jax.ShapeDtypeStruct(full, BF16),
            jax.ShapeDtypeStruct((tile, tile), F32),
        ),
        in_specs=[whole(pltpu.SMEM)] + [whole()] * 6,
        out_specs=(whole(),) * 3,
        scratch_shapes=[pltpu.VMEM((width, width), F32)] * 3,
        compiler_params=pltpu.CompilerParams(vmem_limit_bytes=48 << 20),
        cost_estimate=estimate(35, 1 << 20),
        name="lead_third",
    )(spot, lower0, inverse0, left, work, lower, inverse)


def pack_kernel(count, capacity, source, tiles, lines, *rest):
    buckets, (held, in_sems, out_sems, line_sems) = rest[:count], rest[count:]
    loads, stores = [], []
    tile = tiles.shape[1]
    for k in range(count):
        buckets_end = buckets[k].at[pl.ds(capacity * tile, 16)]
        stores.append(pltpu.make_async_copy(lines.at[k], buckets_end, line_sems.at[k]))
        stores[k].start()
    for n in range(count * capacity):
        loads.append(pltpu.make_async_copy(tiles.at[source[n]], held.at[n], in_sems.at[n]))
        into = buckets[n // capacity].at[pl.ds(n % capacity * tile, tile)]
        stores.append(pltpu.make_async_copy(held.at[n], into, out_sems.at[n]))
    for load in loads:
        load.start()
    for load, store in zip(loads, stores[count:]):
        load.wait()
        store.start()
    for store in stores:
        store.wait()


def route_tiles(contributions, target_front, target_row, target_col, live_count, lead, tile_cols, n_front, n_row, n_col):
    slots = contributions.shape[3]
    tile = contributions.shape[4]
    tiles = contributions.reshape(slots, tile, tile)
    fronts_to = target_front.reshape(slots)
    rows_to = target_row.reshape(slots)
    cols_to = target_col.reshape(slots)
    ids = jnp.arange(slots, dtype=jnp.int32)
    live = ids < live_count.reshape(())
    count = n_front * n_row
    capacity = max(2, -(-slots // count))
    me = lax.axis_index("front") * n_row + lax.axis_index("row")
    local_tile = rows_to // n_row * tile_cols + cols_to // n_col
    bucket_of = jnp.bitwise_xor(fronts_to * n_row + rows_to % n_row, me)
    earlier = (bucket_of[:, None] == bucket_of[None, :]) & live[None, :] & (ids[None, :] < ids[:, None])
    place = bucket_of * capacity + jnp.sum(earlier.astype(jnp.int32), axis=1)
    matches = (place[None, :] == jnp.arange(count * capacity, dtype=jnp.int32)[:, None]) & live[None, :]
    source = jnp.sum(jnp.where(matches, ids[None, :], 0), axis=1)
    filled = jnp.any(matches, axis=1)
    targets = jnp.sum(jnp.where(matches, local_tile[None, :], 0), axis=1)
    targets = jnp.where(filled, targets, -1).astype(BF16).reshape(count, 1, capacity)
    lines = jnp.pad(targets, ((0, 0), (0, 15), (0, tile - capacity)))
    buckets = pl.pallas_call(
        functools.partial(pack_kernel, count, capacity),
        out_shape=tuple(jax.ShapeDtypeStruct((capacity * tile + 16, tile), BF16) for _ in range(count)),
        in_specs=[whole(pltpu.SMEM), whole(pl.ANY), whole(pl.ANY)],
        out_specs=tuple(whole(pl.ANY) for _ in range(count)),
        scratch_shapes=[
            pltpu.VMEM((count * capacity, tile, tile), BF16),
            pltpu.SemaphoreType.DMA((count * capacity,)),
            pltpu.SemaphoreType.DMA((count * capacity,)),
            pltpu.SemaphoreType.DMA((count,)),
        ],
        compiler_params=pltpu.CompilerParams(vmem_limit_bytes=16 << 20),
        cost_estimate=estimate(5, 2 * slots * tile * tile * 2),
        name="pack",
    )(source, tiles, lines)
    buckets, lead = lax.optimization_barrier((buckets, lead))
    axes = ("front", "row")
    received = [buckets[0]]
    for k in range(1, count):
        received.append(lax.ppermute(buckets[k], axes, [(i, i ^ k) for i in range(count)]))
    arrived = jnp.stack([bucket[capacity * tile, :capacity] for bucket in received])
    arrived = arrived.astype(jnp.int32).reshape(-1)
    return received, arrived, lead


def extend_kernel(count, capacity, tile_cols, first, arrived, front, *rest):
    received, out = rest[:count], rest[count]
    row = pl.program_id(0)
    tile = front.shape[2]
    last = first + out.shape[1]
    out[...] = front[:, first:last].astype(F32)
    for k in range(count):
        for p in range(capacity):
            target = arrived[k * capacity + p]
            column = target % tile_cols

            @pl.when(
                (target >= 0) & (target // tile_cols == row) & (column >= first) & (column < last)
            )
            def _():
                out[0, column - first] += received[k][p * tile : (p + 1) * tile, :].astype(F32)


def extend(front, received, arrived, first, last, name):
    rows, tile_cols, tile, _ = front.shape
    cols = last - first
    count, capacity = len(received), received[0].shape[0] // tile
    return pl.pallas_call(
        functools.partial(extend_kernel, count, capacity, tile_cols, first),
        out_shape=jax.ShapeDtypeStruct((rows, cols, tile, tile), F32),
        grid=(rows,),
        in_specs=[whole(pltpu.SMEM), pl.BlockSpec((1, last, tile, tile), lambda a: (a, 0, 0, 0))]
        + [whole()] * count,
        out_specs=pl.BlockSpec((1, cols, tile, tile), lambda a: (a, 0, 0, 0)),
        compiler_params=pltpu.CompilerParams(vmem_limit_bytes=48 << 20),
        cost_estimate=estimate(2 * cols, rows * last * tile * tile * 6),
        name=name,
    )(arrived, front, *received)


def solve_rows(coded, scales, index, t, high, low, tile):
    start = pl.multiple_of(t * tile, tile)
    parts = []
    for c in range(LEAD):
        k = jnp.bitwise_xor(index, c)
        values = coded[k, pl.ds(start, tile), :].astype(jnp.int32).astype(F32)
        parts.append(split(values * scales[k, t]))
    solved = []
    for n in range(LEAD):
        total = None
        for c in range(n + 1):
            rows = slice(n * tile, (n + 1) * tile)
            cols = slice(c * tile, (c + 1) * tile)
            term = mm3_nt(parts[c], (high[rows, cols], low[rows, cols]))
            total = term if total is None else total + term
        solved.append(total)
    return solved


def trailing_kernel(
    tile, n_row, n_col, tile_cols, row0, col0, spot, row_scales, col_scales, panel, work, by_row, by_col, high, low, own, out, cols_hi, cols_lo, rows_f
):
    a = pl.program_id(0)
    row_index, col_index = spot[0], spot[1]
    pieces = tile // LANES

    @pl.when(a == 0)
    def _():
        def body(b, carry):
            start = pl.multiple_of(b * tile, tile)
            solved = solve_rows(by_col, col_scales, row_index, b, high, low, tile)
            for n in range(LEAD):
                hi, lo = split(solved[n])
                cols_hi[pl.ds(start, tile), n * tile : (n + 1) * tile] = hi
                cols_lo[pl.ds(start, tile), n * tile : (n + 1) * tile] = lo
            return carry

        lax.fori_loop(0, tile_cols - col0, body, 0)

    global_row = a * n_row + row_index
    below = global_row >= LEAD

    def finish(b, value):
        for part in range(pieces):
            lanes = value[:, part * LANES : (part + 1) * LANES]
            out[pl.ds(b * pieces + part, tile, stride=tile_cols * pieces), :] = lanes

    @pl.when(below)
    def _():
        solved = solve_rows(by_row, row_scales, col_index, a - row0, high, low, tile)
        for n in range(LEAD):
            rows_f[n] = solved[n]
        rows = split(jnp.concatenate(solved, axis=1))
        for b in range(tile_cols):
            global_col = b * n_col + col_index
            if b * n_col < LEAD:

                @pl.when(global_col < LEAD)
                def _():
                    finish(b, rows_f[jnp.minimum(global_col, LEAD - 1)])

            if b * n_col + n_col > LEAD:

                @pl.when((global_col >= LEAD) & (global_col <= global_row))
                def _():
                    at = slice((b - col0) * tile, (b - col0 + 1) * tile)
                    update = mm3_nt(rows, (cols_hi[at, :], cols_lo[at, :]))
                    finish(b, (work[0, b - 1] if b else panel[0, 0]) - update)

                @pl.when((global_col >= LEAD) & (global_col > global_row))
                def _():
                    finish(b, jnp.zeros((tile, tile), F32))

    @pl.when(jnp.logical_not(below))
    def _():
        for b in range(tile_cols):
            finish(b, jnp.zeros((tile, tile), F32))

        @pl.when((col_index < LEAD) & (col_index <= row_index))
        def _():
            finish(0, own[...])


def trailing(panel, work, by_row, by_col, high, low, own, spot, tile, n_row, n_col, tile_rows, tile_cols, row0, col0):
    cols = tile_cols * tile
    width = LEAD * tile
    count = (tile_cols - col0) * tile
    lines = tile * cols // LANES
    return pl.pallas_call(
        functools.partial(trailing_kernel, tile, n_row, n_col, tile_cols, row0, col0),
        out_shape=jax.ShapeDtypeStruct((tile_rows * lines, LANES), F32),
        grid=(tile_rows,),
        in_specs=[whole(pltpu.SMEM)] * 3
        + [pl.BlockSpec((1, 1, tile, tile), lambda a: (a, 0, 0, 0))]
        + [pl.BlockSpec((1, tile_cols - 1, tile, tile), lambda a: (a, 0, 0, 0))]
        + [whole()] * 5,
        out_specs=pl.BlockSpec((lines, LANES), lambda a: (a, 0)),
        scratch_shapes=[
            pltpu.VMEM((count, width), BF16),
            pltpu.VMEM((count, width), BF16),
            pltpu.VMEM((LEAD, tile, tile), F32),
        ],
        compiler_params=pltpu.CompilerParams(vmem_limit_bytes=56 << 20),
        cost_estimate=estimate(25, tile_rows * lines * LANES * 8),
        name="trailing",
    )(spot, decode_scales(by_row, tile), decode_scales(by_col, tile), panel, work, by_row, by_col, high, low, own)


def encode(piece, tile):
    tiles = piece.reshape(-1, tile, tile)
    largest = jnp.max(jnp.abs(tiles), axis=(1, 2))
    power = jnp.floor(jnp.log2(jnp.maximum(largest, 1e-30))) + 1.0
    half = jnp.floor(0.5 * power)
    shrunk = tiles * jnp.exp2(-half)[:, None, None]
    codes = jnp.round(shrunk * (jnp.exp2(half - power) * TOP)[:, None, None]).astype(jnp.int16)
    line = jnp.zeros((16, tile), jnp.int16).at[0, : tiles.shape[0]].set(power.astype(jnp.int16))
    return jnp.concatenate([codes.reshape(-1, tile), line], axis=0)


def decode_scales(coded, tile):
    rows = coded.shape[1] - 16
    return jnp.exp2(coded[:, rows, : rows // tile].astype(F32) - 14.0) * (16384.0 / TOP)


def exchange(piece, axis, size):
    return [piece] + [
        lax.ppermute(piece, axis, [(i, i ^ k) for i in range(size)]) for k in range(1, size)
    ]


def per_device(front_matrix, contributions, target_front, target_row, target_col, live_count):
    tile_rows = front_matrix.shape[1]
    tile = front_matrix.shape[3]
    tile_cols = front_matrix.shape[4]
    n_front = lax.axis_size("front")
    n_row = lax.axis_size("row")
    n_col = lax.axis_size("col")
    spot = jnp.stack([lax.axis_index("row"), lax.axis_index("col")]).astype(jnp.int32)
    row0, col0 = LEAD // n_row, LEAD // n_col

    line = jnp.stack(exchange(front_matrix[0, 0, 0, :, 0, 0, :], "col", n_col))
    lead = exchange(line, "row", n_row)
    front = front_matrix.reshape(tile_rows, tile, tile_cols, tile).transpose(0, 2, 1, 3)
    received, arrived, lead = route_tiles(
        contributions, target_front, target_row, target_col, live_count, lead, tile_cols, n_front, n_row, n_col
    )
    lower0, inverse0 = lead_first(lead, spot, tile)
    arrived, lower0 = lax.optimization_barrier((arrived, lower0))
    panel = extend(front, received, arrived, 0, 1, "extend_panel")
    coded = encode(panel[row0:, 0].reshape(-1, tile), tile)
    by_row = exchange(coded, "col", n_col)
    mirrored = lax.ppermute(
        coded,
        ("row", "col"),
        [(r * n_col + c, c * n_col + r) for r in range(n_row) for c in range(n_col)],
    )
    work = extend(front, received, arrived, 1, tile_cols, "extend_rest")
    left, work1, lower1, inverse1 = lead_second(lead, inverse0, spot, tile)
    mirrored, work1 = lax.optimization_barrier((mirrored, work1))
    by_col = exchange(mirrored, "row", n_row)
    high, low, own = lead_third(lower0, inverse0, left, work1, lower1, inverse1, spot, tile)
    factor = trailing(
        panel,
        work,
        jnp.stack(by_row),
        jnp.stack(by_col),
        high,
        low,
        own,
        spot,
        tile,
        n_row,
        n_col,
        tile_rows,
        tile_cols,
        row0,
        col0,
    )
    return factor.reshape(1, tile_rows, 1, tile, tile_cols, 1, tile)


def solution(mesh):
    in_specs = (
        P("front", None, "row", None, None, "col", None),
        P("front", "row", "col", None, None, None),
        P("front", "row", "col", None),
        P("front", "row", "col", None),
        P("front", "row", "col", None),
        P("front", "row", "col"),
    )
    out_specs = P("front", None, "row", None, None, "col", None)
    return jax.shard_map(
        per_device, mesh=mesh, in_specs=in_specs, out_specs=out_specs, check_vma=False
    )
```

```python
import functools

import jax
import jax.numpy as jnp
from jax import lax
from jax.experimental import pallas as pl
from jax.experimental.pallas import tpu as pltpu
from jax.sharding import PartitionSpec as P

PANEL_TILES = 2
PANELS = 2
LEAD = PANEL_TILES * PANELS
BLOCK = 128
LANES = 128
TOP = 32000.0
HIGHEST = lax.Precision.HIGHEST
NT = (((1,), (1,)), ((), ()))
F32 = jnp.float32
BF16 = jnp.bfloat16


def mm(a, b):
    return jnp.dot(a, b, precision=HIGHEST, preferred_element_type=F32)


def mm_nt(a, b):
    return lax.dot_general(a, b, NT, precision=HIGHEST, preferred_element_type=F32)


def split(x):
    hi = x.astype(BF16)
    return hi, (x - hi.astype(F32)).astype(BF16)


def mm3_nt(a, b):
    (ah, al), (bh, bl) = a, b
    one = functools.partial(lax.dot_general, dimension_numbers=NT, preferred_element_type=F32)
    return one(ah, bh) + (one(ah, bl) + one(al, bh))


def eliminate(block):
    groups = BLOCK // 8
    upper = [block[8 * i : 8 * i + 8, :] for i in range(groups)]
    rows = lax.broadcasted_iota(jnp.int32, (8, BLOCK), 0)
    lanes = lax.broadcasted_iota(jnp.int32, (8, BLOCK), 1)
    inverse = [jnp.where(rows + 8 * i == lanes, 1.0, 0.0).astype(F32) for i in range(groups)]
    sub = lax.broadcasted_iota(jnp.int32, (8, 1), 0)
    for j in range(BLOCK):
        g, s = divmod(j, 8)
        row_u = upper[g][s : s + 1, :]
        row_i = inverse[g][s : s + 1, :]
        scale = 1.0 / row_u[:, j : j + 1]
        row_u = row_u * scale
        row_i = row_i * scale
        for i in range(g, groups):
            column = upper[i][:, j : j + 1]
            if i == g:
                if s == 7:
                    continue
                column = jnp.where(sub > s, column, 0.0)
            upper[i] = upper[i] - column * row_u
            inverse[i] = inverse[i] - column * row_i
    return jnp.concatenate(upper, axis=0), jnp.concatenate(inverse, axis=0)


def set_eye(ref):
    ids = lax.broadcasted_iota(jnp.int32, ref.shape, 0)
    ref[...] = jnp.where(ids == lax.broadcasted_iota(jnp.int32, ref.shape, 1), 1.0, 0.0).astype(F32)


def factor_panel(work, lower, inverse, first, last):
    size = work.shape[0]
    row_ids = lax.broadcasted_iota(jnp.int32, (size, BLOCK), 0)
    eye = lax.broadcasted_iota(jnp.int32, (BLOCK, BLOCK), 0) == lax.broadcasted_iota(
        jnp.int32, (BLOCK, BLOCK), 1
    )
    above = lax.broadcasted_iota(jnp.int32, (BLOCK, BLOCK), 0) <= lax.broadcasted_iota(
        jnp.int32, (BLOCK, BLOCK), 1
    )

    def step(k, carry):
        start = pl.multiple_of(k * BLOCK, BLOCK)
        here = pl.ds(start, BLOCK)
        upper, unit = eliminate(work[here, here])
        diagonal = jnp.sum(jnp.where(eye, upper, 0.0), axis=1, keepdims=True)
        root = lax.rsqrt(diagonal)
        root = root * (1.5 - 0.5 * diagonal * root * root)
        small = unit * root
        column = mm_nt(work[:, here], small)
        below = jnp.where(row_ids >= start + BLOCK, column, 0.0)
        lower[:, here] = below
        lower[here, here] = jnp.where(above, upper * root, 0.0).T
        solved = mm(small, inverse[here, :])
        inverse[here, :] = solved
        work[...] -= mm_nt(below, below)
        inverse[...] -= mm(below, solved)
        return carry

    lax.fori_loop(first, last, step, 0)


def load_square(spot, lead, work, row0, col0, tile):
    for k, tiles in enumerate(lead):
        row = jnp.bitwise_xor(spot[0], k) - row0

        @pl.when((row >= 0) & (row < PANEL_TILES))
        def _():
            at = pl.ds(pl.multiple_of(row * tile, tile), tile)
            for j in range(PANEL_TILES):
                place = jnp.bitwise_xor(spot[1], col0 + j)
                work[at, j * tile : (j + 1) * tile] = tiles[place].astype(F32)


def first_kernel(tile, n_row, spot, *rest):
    lead, (lower, inverse, work) = rest[:n_row], rest[n_row:]
    load_square(spot, lead, work, 0, 0, tile)
    set_eye(inverse)
    factor_panel(work, lower, inverse, 0, work.shape[0] // BLOCK)


def second_kernel(tile, n_row, spot, *rest):
    lead, (inverse0, left, work, lower, inverse) = rest[:n_row], rest[n_row:]
    load_square(spot, lead, work, PANEL_TILES, 0, tile)
    left[...] = mm_nt(work[...], inverse0[...])
    load_square(spot, lead, work, PANEL_TILES, PANEL_TILES, tile)
    work[...] -= mm_nt(left[...], left[...])
    set_eye(inverse)
    lower[...] = jnp.zeros_like(lower)
    factor_panel(work, lower, inverse, 0, work.shape[0] // BLOCK // 2)


def third_kernel(tile, spot, lower0, inverse0, left, work1, lower1, inverse1, high, low, own, work, lower, inverse):
    width = PANEL_TILES * tile
    work[...] = work1[...]
    lower[...] = lower1[...]
    inverse[...] = inverse1[...]
    blocks = width // BLOCK
    factor_panel(work, lower, inverse, blocks // 2, blocks)
    corner = -mm(inverse[...], mm(left[...], inverse0[...]))
    for r, c, value in (
        (0, 0, inverse0[...]),
        (0, 1, jnp.zeros((width, width), F32)),
        (1, 0, corner),
        (1, 1, inverse[...]),
    ):
        hi, lo = split(value)
        high[r * width : (r + 1) * width, c * width : (c + 1) * width] = hi
        low[r * width : (r + 1) * width, c * width : (c + 1) * width] = lo
    own[...] = jnp.zeros_like(own)
    for r, c, square in ((0, 0, lower0), (1, 0, left), (1, 1, lower)):
        row, col = spot[0] - r * PANEL_TILES, spot[1] - c * PANEL_TILES

        @pl.when((row >= 0) & (row < PANEL_TILES) & (col >= 0) & (col < PANEL_TILES))
        def _():
            own[...] = square[
                pl.ds(pl.multiple_of(row * tile, tile), tile),
                pl.ds(pl.multiple_of(col * tile, tile), tile),
            ]


def whole(space=pltpu.VMEM):
    return pl.BlockSpec(memory_space=space)


def estimate(us, size):
    return pl.CostEstimate(flops=int(us * 1e9), bytes_accessed=size, transcendentals=0)


def lead_first(lead, spot, tile):
    width = PANEL_TILES * tile
    square = jax.ShapeDtypeStruct((width, width), F32)
    return pl.pallas_call(
        functools.partial(first_kernel, tile, len(lead)),
        out_shape=(square, square),
        in_specs=[whole(pltpu.SMEM)] + [whole()] * len(lead),
        out_specs=(whole(), whole()),
        scratch_shapes=[pltpu.VMEM((width, width), F32)],
        compiler_params=pltpu.CompilerParams(vmem_limit_bytes=48 << 20),
        cost_estimate=estimate(60, 1 << 20),
        name="lead_first",
    )(spot, *lead)


def lead_second(lead, inverse0, spot, tile):
    width = PANEL_TILES * tile
    square = jax.ShapeDtypeStruct((width, width), F32)
    return pl.pallas_call(
        functools.partial(second_kernel, tile, len(lead)),
        out_shape=(square,) * 4,
        in_specs=[whole(pltpu.SMEM)] + [whole()] * (len(lead) + 1),
        out_specs=(whole(),) * 4,
        compiler_params=pltpu.CompilerParams(vmem_limit_bytes=48 << 20),
        cost_estimate=estimate(30, 1 << 20),
        name="lead_second",
    )(spot, *lead, inverse0)


def lead_third(lower0, inverse0, left, work, lower, inverse, spot, tile):
    width = PANEL_TILES * tile
    full = (2 * width, 2 * width)
    return pl.pallas_call(
        functools.partial(third_kernel, tile),
        out_shape=(
            jax.ShapeDtypeStruct(full, BF16),
            jax.ShapeDtypeStruct(full, BF16),
            jax.ShapeDtypeStruct((tile, tile), F32),
        ),
        in_specs=[whole(pltpu.SMEM)] + [whole()] * 6,
        out_specs=(whole(),) * 3,
        scratch_shapes=[pltpu.VMEM((width, width), F32)] * 3,
        compiler_params=pltpu.CompilerParams(vmem_limit_bytes=48 << 20),
        cost_estimate=estimate(35, 1 << 20),
        name="lead_third",
    )(spot, lower0, inverse0, left, work, lower, inverse)


def pack_kernel(count, capacity, source, tiles, lines, *rest):
    near, (far, held, in_sems, out_sems, line_sems) = rest[:-5], rest[-5:]
    tile = tiles.shape[1]
    segment = capacity * tile + 16

    def place(k, start, size):
        if k < len(near):
            return near[k].at[pl.ds(start, size)]
        return far.at[pl.ds((k - len(near)) * segment + start, size)]

    tails, loads, stores = [], [], []
    for k in range(count):
        into = place(k, capacity * tile, 16)
        tails.append(pltpu.make_async_copy(lines.at[k], into, line_sems.at[k]))
    for n in range(count * capacity):
        loads.append(pltpu.make_async_copy(tiles.at[source[n]], held.at[n], in_sems.at[n]))
        into = place(n // capacity, n % capacity * tile, tile)
        stores.append(pltpu.make_async_copy(held.at[n], into, out_sems.at[n]))
    for load in loads:
        load.start()
    for tail in tails:
        tail.start()
    for load, store in zip(loads, stores):
        load.wait()
        store.start()
    for store in stores:
        store.wait()
    for tail in tails:
        tail.wait()


def route_tiles(contributions, target_front, target_row, target_col, live_count, lead, tile_cols, n_front, n_row, n_col):
    slots = contributions.shape[3]
    tile = contributions.shape[4]
    tiles = contributions.reshape(slots, tile, tile)
    fronts_to = target_front.reshape(slots)
    rows_to = target_row.reshape(slots)
    cols_to = target_col.reshape(slots)
    ids = jnp.arange(slots, dtype=jnp.int32)
    live = ids < live_count.reshape(())
    count = n_front * n_row
    capacity = max(2, -(-slots // count))
    me = lax.axis_index("front") * n_row + lax.axis_index("row")
    local_tile = rows_to // n_row * tile_cols + cols_to // n_col
    bucket_of = jnp.bitwise_xor(fronts_to * n_row + rows_to % n_row, me)
    earlier = (bucket_of[:, None] == bucket_of[None, :]) & live[None, :] & (ids[None, :] < ids[:, None])
    place = bucket_of * capacity + jnp.sum(earlier.astype(jnp.int32), axis=1)
    matches = (place[None, :] == jnp.arange(count * capacity, dtype=jnp.int32)[:, None]) & live[None, :]
    source = jnp.sum(jnp.where(matches, ids[None, :], 0), axis=1)
    filled = jnp.any(matches, axis=1)
    targets = jnp.sum(jnp.where(matches, local_tile[None, :], 0), axis=1)
    targets = jnp.where(filled, targets, -1).astype(BF16).reshape(count, 1, capacity)
    lines = jnp.pad(targets, ((0, 0), (0, 15), (0, tile - capacity)))
    segment = capacity * tile + 16
    packed = pl.pallas_call(
        functools.partial(pack_kernel, count, capacity),
        out_shape=tuple(jax.ShapeDtypeStruct((segment, tile), BF16) for _ in range(n_row))
        + (jax.ShapeDtypeStruct(((count - n_row) * segment, tile), BF16),),
        in_specs=[whole(pltpu.SMEM), whole(pl.ANY), whole(pl.ANY)],
        out_specs=tuple(whole(pl.ANY) for _ in range(n_row + 1)),
        scratch_shapes=[
            pltpu.VMEM((count * capacity, tile, tile), BF16),
            pltpu.SemaphoreType.DMA((count * capacity,)),
            pltpu.SemaphoreType.DMA((count * capacity,)),
            pltpu.SemaphoreType.DMA((count,)),
        ],
        compiler_params=pltpu.CompilerParams(vmem_limit_bytes=16 << 20),
        cost_estimate=estimate(5, 2 * slots * tile * tile * 2),
        name="pack",
    )(source, tiles, lines)
    near, far = packed[:n_row], packed[n_row]
    far = far.reshape(n_front - 1, n_row, segment, tile)
    others = [
        lax.ppermute(far[f - 1], "front", [(i, i ^ f) for i in range(n_front)])
        for f in range(1, n_front)
    ]
    groups = [jnp.concatenate([near[k]] + [other[k] for other in others]) for k in range(n_row)]
    groups, lead = lax.optimization_barrier((groups, lead))
    received = [groups[0]] + [
        lax.ppermute(groups[k], "row", [(i, i ^ k) for i in range(n_row)]) for k in range(1, n_row)
    ]
    arrived = jnp.stack(
        [group.reshape(n_front, segment, tile)[:, capacity * tile, :capacity] for group in received]
    )
    arrived = arrived.astype(jnp.int32).reshape(-1)
    return received, arrived, lead


def extend_kernel(groups, parts, capacity, tile_cols, first, arrived, front, *rest):
    received, out = rest[:groups], rest[groups]
    row = pl.program_id(0)
    tile = front.shape[2]
    last = first + out.shape[1]
    segment = capacity * tile + 16
    out[...] = front[:, first:last].astype(F32)
    for k in range(groups):
        for part in range(parts):
            for p in range(capacity):
                target = arrived[(k * parts + part) * capacity + p]
                column = target % tile_cols
                start = part * segment + p * tile

                @pl.when(
                    (target >= 0) & (target // tile_cols == row) & (column >= first) & (column < last)
                )
                def _():
                    out[0, column - first] += received[k][start : start + tile, :].astype(F32)


def extend(front, received, arrived, capacity, first, last, name):
    rows, tile_cols, tile, _ = front.shape
    cols = last - first
    count = len(received)
    parts = received[0].shape[0] // (capacity * tile + 16)
    return pl.pallas_call(
        functools.partial(extend_kernel, count, parts, capacity, tile_cols, first),
        out_shape=jax.ShapeDtypeStruct((rows, cols, tile, tile), F32),
        grid=(rows,),
        in_specs=[whole(pltpu.SMEM), pl.BlockSpec((1, last, tile, tile), lambda a: (a, 0, 0, 0))]
        + [whole()] * count,
        out_specs=pl.BlockSpec((1, cols, tile, tile), lambda a: (a, 0, 0, 0)),
        compiler_params=pltpu.CompilerParams(vmem_limit_bytes=48 << 20),
        cost_estimate=estimate(2 * cols, rows * last * tile * tile * 6),
        name=name,
    )(arrived, front, *received)


def solve_rows(coded, scales, index, t, high, low, tile):
    start = pl.multiple_of(t * tile, tile)
    parts = []
    for c in range(LEAD):
        k = jnp.bitwise_xor(index, c)
        values = coded[k, pl.ds(start, tile), :].astype(jnp.int32).astype(F32)
        parts.append(split(values * scales[k, t]))
    solved = []
    for n in range(LEAD):
        total = None
        for c in range(n + 1):
            rows = slice(n * tile, (n + 1) * tile)
            cols = slice(c * tile, (c + 1) * tile)
            term = mm3_nt(parts[c], (high[rows, cols], low[rows, cols]))
            total = term if total is None else total + term
        solved.append(total)
    return solved


def trailing_kernel(
    tile, n_row, n_col, tile_cols, row0, col0, spot, row_scales, col_scales, panel, work, by_row, by_col, high, low, own, out, cols_hi, cols_lo, rows_f
):
    a = pl.program_id(0)
    row_index, col_index = spot[0], spot[1]
    pieces = tile // LANES

    @pl.when(a == 0)
    def _():
        def body(b, carry):
            start = pl.multiple_of(b * tile, tile)
            solved = solve_rows(by_col, col_scales, row_index, b, high, low, tile)
            for n in range(LEAD):
                hi, lo = split(solved[n])
                cols_hi[pl.ds(start, tile), n * tile : (n + 1) * tile] = hi
                cols_lo[pl.ds(start, tile), n * tile : (n + 1) * tile] = lo
            return carry

        lax.fori_loop(0, tile_cols - col0, body, 0)

    global_row = a * n_row + row_index
    below = global_row >= LEAD

    def finish(b, value):
        for part in range(pieces):
            lanes = value[:, part * LANES : (part + 1) * LANES]
            out[pl.ds(b * pieces + part, tile, stride=tile_cols * pieces), :] = lanes

    @pl.when(below)
    def _():
        solved = solve_rows(by_row, row_scales, col_index, a - row0, high, low, tile)
        for n in range(LEAD):
            rows_f[n] = solved[n]
        rows = split(jnp.concatenate(solved, axis=1))
        for b in range(tile_cols):
            global_col = b * n_col + col_index
            if b * n_col < LEAD:

                @pl.when(global_col < LEAD)
                def _():
                    finish(b, rows_f[jnp.minimum(global_col, LEAD - 1)])

            if b * n_col + n_col > LEAD:

                @pl.when((global_col >= LEAD) & (global_col <= global_row))
                def _():
                    at = slice((b - col0) * tile, (b - col0 + 1) * tile)
                    update = mm3_nt(rows, (cols_hi[at, :], cols_lo[at, :]))
                    finish(b, (work[0, b - 1] if b else panel[0, 0]) - update)

                @pl.when((global_col >= LEAD) & (global_col > global_row))
                def _():
                    finish(b, jnp.zeros((tile, tile), F32))

    @pl.when(jnp.logical_not(below))
    def _():
        for b in range(tile_cols):
            finish(b, jnp.zeros((tile, tile), F32))

        @pl.when((col_index < LEAD) & (col_index <= row_index))
        def _():
            finish(0, own[...])


def trailing(panel, work, by_row, by_col, high, low, own, spot, tile, n_row, n_col, tile_rows, tile_cols, row0, col0):
    cols = tile_cols * tile
    width = LEAD * tile
    count = (tile_cols - col0) * tile
    lines = tile * cols // LANES
    return pl.pallas_call(
        functools.partial(trailing_kernel, tile, n_row, n_col, tile_cols, row0, col0),
        out_shape=jax.ShapeDtypeStruct((tile_rows * lines, LANES), F32),
        grid=(tile_rows,),
        in_specs=[whole(pltpu.SMEM)] * 3
        + [pl.BlockSpec((1, 1, tile, tile), lambda a: (a, 0, 0, 0))]
        + [pl.BlockSpec((1, tile_cols - 1, tile, tile), lambda a: (a, 0, 0, 0))]
        + [whole()] * 5,
        out_specs=pl.BlockSpec((lines, LANES), lambda a: (a, 0)),
        scratch_shapes=[
            pltpu.VMEM((count, width), BF16),
            pltpu.VMEM((count, width), BF16),
            pltpu.VMEM((LEAD, tile, tile), F32),
        ],
        compiler_params=pltpu.CompilerParams(vmem_limit_bytes=56 << 20),
        cost_estimate=estimate(25, tile_rows * lines * LANES * 8),
        name="trailing",
    )(spot, decode_scales(by_row, tile), decode_scales(by_col, tile), panel, work, by_row, by_col, high, low, own)


def encode(piece, tile):
    tiles = piece.reshape(-1, tile, tile)
    largest = jnp.max(jnp.abs(tiles), axis=(1, 2))
    power = jnp.floor(jnp.log2(jnp.maximum(largest, 1e-30))) + 1.0
    half = jnp.floor(0.5 * power)
    shrunk = tiles * jnp.exp2(-half)[:, None, None]
    codes = jnp.round(shrunk * (jnp.exp2(half - power) * TOP)[:, None, None]).astype(jnp.int16)
    line = jnp.zeros((16, tile), jnp.int16).at[0, : tiles.shape[0]].set(power.astype(jnp.int16))
    return jnp.concatenate([codes.reshape(-1, tile), line], axis=0)


def decode_scales(coded, tile):
    rows = coded.shape[1] - 16
    return jnp.exp2(coded[:, rows, : rows // tile].astype(F32) - 14.0) * (16384.0 / TOP)


def partner(piece, axis, size, k):
    return lax.ppermute(piece, axis, [(i, i ^ k) for i in range(size)])


def exchange(piece, axis, size, first=1):
    return [partner(piece, axis, size, k) for k in range(first, size)]


def per_device(front_matrix, contributions, target_front, target_row, target_col, live_count):
    tile_rows = front_matrix.shape[1]
    tile = front_matrix.shape[3]
    tile_cols = front_matrix.shape[4]
    n_front = lax.axis_size("front")
    n_row = lax.axis_size("row")
    n_col = lax.axis_size("col")
    spot = jnp.stack([lax.axis_index("row"), lax.axis_index("col")]).astype(jnp.int32)
    row0, col0 = LEAD // n_row, LEAD // n_col

    line = front_matrix[0, 0, 0, :, 0, 0, :]
    line = jnp.stack([line] + exchange(line, "col", n_col))
    lead = [line] + exchange(line, "row", n_row)
    front = front_matrix.reshape(tile_rows, tile, tile_cols, tile).transpose(0, 2, 1, 3)
    capacity = max(2, -(-contributions.shape[3] // (n_front * n_row)))
    received, arrived, lead = route_tiles(
        contributions, target_front, target_row, target_col, live_count, lead, tile_cols, n_front, n_row, n_col
    )
    lower0, inverse0 = lead_first(lead, spot, tile)
    arrived, lower0 = lax.optimization_barrier((arrived, lower0))
    panel = extend(front, received, arrived, capacity, 0, 1, "extend_panel")
    coded = encode(panel[row0:, 0].reshape(-1, tile), tile)
    coded, inverse0 = lax.optimization_barrier((coded, inverse0))
    mirrored = lax.ppermute(
        coded,
        ("row", "col"),
        [(r * n_col + c, c * n_col + r) for r in range(n_row) for c in range(n_col)],
    )
    work = extend(front, received, arrived, capacity, 1, tile_cols, "extend_rest")
    left, work1, lower1, inverse1 = lead_second(lead, inverse0, spot, tile)
    beside = partner(coded, "col", n_col, 1)
    mirrored, coded, work1 = lax.optimization_barrier((mirrored, coded, work1))
    by_row = [coded, beside] + exchange(coded, "col", n_col, 2)
    by_col = [mirrored] + exchange(mirrored, "row", n_row)
    high, low, own = lead_third(lower0, inverse0, left, work1, lower1, inverse1, spot, tile)
    factor = trailing(
        panel,
        work,
        jnp.stack(by_row),
        jnp.stack(by_col),
        high,
        low,
        own,
        spot,
        tile,
        n_row,
        n_col,
        tile_rows,
        tile_cols,
        row0,
        col0,
    )
    return factor.reshape(1, tile_rows, 1, tile, tile_cols, 1, tile)


def solution(mesh):
    in_specs = (
        P("front", None, "row", None, None, "col", None),
        P("front", "row", "col", None, None, None),
        P("front", "row", "col", None),
        P("front", "row", "col", None),
        P("front", "row", "col", None),
        P("front", "row", "col"),
    )
    out_specs = P("front", None, "row", None, None, "col", None)
    return jax.shard_map(
        per_device, mesh=mesh, in_specs=in_specs, out_specs=out_specs, check_vma=False
    )
```

```python
import functools

import jax
import jax.numpy as jnp
from jax import lax
from jax.experimental import pallas as pl
from jax.experimental.pallas import tpu as pltpu
from jax.sharding import PartitionSpec as P

PANEL_TILES = 2
PANELS = 2
LEAD = PANEL_TILES * PANELS
BLOCK = 128
LANES = 128
TOP = 32000.0
HIGHEST = lax.Precision.HIGHEST
NT = (((1,), (1,)), ((), ()))
F32 = jnp.float32
BF16 = jnp.bfloat16


def mm(a, b):
    return jnp.dot(a, b, precision=HIGHEST, preferred_element_type=F32)


def mm_nt(a, b):
    return lax.dot_general(a, b, NT, precision=HIGHEST, preferred_element_type=F32)


def split(x):
    hi = x.astype(BF16)
    return hi, (x - hi.astype(F32)).astype(BF16)


def mm3_nt(a, b):
    (ah, al), (bh, bl) = a, b
    one = functools.partial(lax.dot_general, dimension_numbers=NT, preferred_element_type=F32)
    return one(ah, bh) + (one(ah, bl) + one(al, bh))


def eliminate(block):
    groups = BLOCK // 8
    upper = [block[8 * i : 8 * i + 8, :] for i in range(groups)]
    rows = lax.broadcasted_iota(jnp.int32, (8, BLOCK), 0)
    lanes = lax.broadcasted_iota(jnp.int32, (8, BLOCK), 1)
    inverse = [jnp.where(rows + 8 * i == lanes, 1.0, 0.0).astype(F32) for i in range(groups)]
    sub = lax.broadcasted_iota(jnp.int32, (8, 1), 0)
    for j in range(BLOCK):
        g, s = divmod(j, 8)
        row_u = upper[g][s : s + 1, :]
        row_i = inverse[g][s : s + 1, :]
        scale = 1.0 / row_u[:, j : j + 1]
        row_u = row_u * scale
        row_i = row_i * scale
        for i in range(g, groups):
            column = upper[i][:, j : j + 1]
            if i == g:
                if s == 7:
                    continue
                column = jnp.where(sub > s, column, 0.0)
            upper[i] = upper[i] - column * row_u
            inverse[i] = inverse[i] - column * row_i
    return jnp.concatenate(upper, axis=0), jnp.concatenate(inverse, axis=0)


def set_eye(ref):
    ids = lax.broadcasted_iota(jnp.int32, ref.shape, 0)
    ref[...] = jnp.where(ids == lax.broadcasted_iota(jnp.int32, ref.shape, 1), 1.0, 0.0).astype(F32)


def factor_panel(work, lower, inverse, first, last):
    size = work.shape[0]
    row_ids = lax.broadcasted_iota(jnp.int32, (size, BLOCK), 0)
    eye = lax.broadcasted_iota(jnp.int32, (BLOCK, BLOCK), 0) == lax.broadcasted_iota(
        jnp.int32, (BLOCK, BLOCK), 1
    )
    above = lax.broadcasted_iota(jnp.int32, (BLOCK, BLOCK), 0) <= lax.broadcasted_iota(
        jnp.int32, (BLOCK, BLOCK), 1
    )

    def step(k, carry):
        start = pl.multiple_of(k * BLOCK, BLOCK)
        here = pl.ds(start, BLOCK)
        upper, unit = eliminate(work[here, here])
        diagonal = jnp.sum(jnp.where(eye, upper, 0.0), axis=1, keepdims=True)
        root = lax.rsqrt(diagonal)
        root = root * (1.5 - 0.5 * diagonal * root * root)
        small = unit * root
        column = mm_nt(work[:, here], small)
        below = jnp.where(row_ids >= start + BLOCK, column, 0.0)
        lower[:, here] = below
        lower[here, here] = jnp.where(above, upper * root, 0.0).T
        solved = mm(small, inverse[here, :])
        inverse[here, :] = solved
        work[...] -= mm_nt(below, below)
        inverse[...] -= mm(below, solved)
        return carry

    lax.fori_loop(first, last, step, 0)


def load_square(spot, lead, work, row0, col0, tile):
    for k, tiles in enumerate(lead):
        row = jnp.bitwise_xor(spot[0], k) - row0

        @pl.when((row >= 0) & (row < PANEL_TILES))
        def _():
            at = pl.ds(pl.multiple_of(row * tile, tile), tile)
            for j in range(PANEL_TILES):
                place = jnp.bitwise_xor(spot[1], col0 + j)
                work[at, j * tile : (j + 1) * tile] = tiles[place].astype(F32)


def first_kernel(tile, n_row, spot, *rest):
    lead, (lower, inverse, work) = rest[:n_row], rest[n_row:]
    load_square(spot, lead, work, 0, 0, tile)
    set_eye(inverse)
    factor_panel(work, lower, inverse, 0, work.shape[0] // BLOCK)


def second_kernel(tile, n_row, spot, *rest):
    lead, (inverse0, left, work, lower, inverse) = rest[:n_row], rest[n_row:]
    load_square(spot, lead, work, PANEL_TILES, 0, tile)
    left[...] = mm_nt(work[...], inverse0[...])
    load_square(spot, lead, work, PANEL_TILES, PANEL_TILES, tile)
    work[...] -= mm_nt(left[...], left[...])
    set_eye(inverse)
    lower[...] = jnp.zeros_like(lower)
    factor_panel(work, lower, inverse, 0, work.shape[0] // BLOCK // 2)


def third_kernel(tile, spot, lower0, inverse0, left, work1, lower1, inverse1, high, low, own, work, lower, inverse):
    width = PANEL_TILES * tile
    work[...] = work1[...]
    lower[...] = lower1[...]
    inverse[...] = inverse1[...]
    blocks = width // BLOCK
    factor_panel(work, lower, inverse, blocks // 2, blocks)
    corner = -mm(inverse[...], mm(left[...], inverse0[...]))
    for r, c, value in (
        (0, 0, inverse0[...]),
        (0, 1, jnp.zeros((width, width), F32)),
        (1, 0, corner),
        (1, 1, inverse[...]),
    ):
        hi, lo = split(value)
        high[r * width : (r + 1) * width, c * width : (c + 1) * width] = hi
        low[r * width : (r + 1) * width, c * width : (c + 1) * width] = lo
    own[...] = jnp.zeros_like(own)
    for r, c, square in ((0, 0, lower0), (1, 0, left), (1, 1, lower)):
        row, col = spot[0] - r * PANEL_TILES, spot[1] - c * PANEL_TILES

        @pl.when((row >= 0) & (row < PANEL_TILES) & (col >= 0) & (col < PANEL_TILES))
        def _():
            own[...] = square[
                pl.ds(pl.multiple_of(row * tile, tile), tile),
                pl.ds(pl.multiple_of(col * tile, tile), tile),
            ]


def whole(space=pltpu.VMEM):
    return pl.BlockSpec(memory_space=space)


def estimate(us, size):
    return pl.CostEstimate(flops=int(us * 1e9), bytes_accessed=size, transcendentals=0)


def lead_first(lead, spot, tile):
    width = PANEL_TILES * tile
    square = jax.ShapeDtypeStruct((width, width), F32)
    return pl.pallas_call(
        functools.partial(first_kernel, tile, len(lead)),
        out_shape=(square, square),
        in_specs=[whole(pltpu.SMEM)] + [whole()] * len(lead),
        out_specs=(whole(), whole()),
        scratch_shapes=[pltpu.VMEM((width, width), F32)],
        compiler_params=pltpu.CompilerParams(vmem_limit_bytes=48 << 20),
        cost_estimate=estimate(60, 1 << 20),
        name="lead_first",
    )(spot, *lead)


def lead_second(lead, inverse0, spot, tile):
    width = PANEL_TILES * tile
    square = jax.ShapeDtypeStruct((width, width), F32)
    return pl.pallas_call(
        functools.partial(second_kernel, tile, len(lead)),
        out_shape=(square,) * 4,
        in_specs=[whole(pltpu.SMEM)] + [whole()] * (len(lead) + 1),
        out_specs=(whole(),) * 4,
        compiler_params=pltpu.CompilerParams(vmem_limit_bytes=48 << 20),
        cost_estimate=estimate(30, 1 << 20),
        name="lead_second",
    )(spot, *lead, inverse0)


def lead_third(lower0, inverse0, left, work, lower, inverse, spot, tile):
    width = PANEL_TILES * tile
    full = (2 * width, 2 * width)
    return pl.pallas_call(
        functools.partial(third_kernel, tile),
        out_shape=(
            jax.ShapeDtypeStruct(full, BF16),
            jax.ShapeDtypeStruct(full, BF16),
            jax.ShapeDtypeStruct((tile, tile), F32),
        ),
        in_specs=[whole(pltpu.SMEM)] + [whole()] * 6,
        out_specs=(whole(),) * 3,
        scratch_shapes=[pltpu.VMEM((width, width), F32)] * 3,
        compiler_params=pltpu.CompilerParams(vmem_limit_bytes=48 << 20),
        cost_estimate=estimate(35, 1 << 20),
        name="lead_third",
    )(spot, lower0, inverse0, left, work, lower, inverse)


def pack_kernel(count, capacity, source, tiles, lines, *rest):
    near, (far, held, in_sems, out_sems, line_sems) = rest[:-5], rest[-5:]
    tile = tiles.shape[1]
    segment = capacity * tile + 16

    def place(k, start, size):
        if k < len(near):
            return near[k].at[pl.ds(start, size)]
        return far.at[pl.ds((k - len(near)) * segment + start, size)]

    tails, loads, stores = [], [], []
    for k in range(count):
        into = place(k, capacity * tile, 16)
        tails.append(pltpu.make_async_copy(lines.at[k], into, line_sems.at[k]))
    for n in range(count * capacity):
        loads.append(pltpu.make_async_copy(tiles.at[source[n]], held.at[n], in_sems.at[n]))
        into = place(n // capacity, n % capacity * tile, tile)
        stores.append(pltpu.make_async_copy(held.at[n], into, out_sems.at[n]))
    for load in loads:
        load.start()
    for tail in tails:
        tail.start()
    for load, store in zip(loads, stores):
        load.wait()
        store.start()
    for store in stores:
        store.wait()
    for tail in tails:
        tail.wait()


def route_tiles(contributions, target_front, target_row, target_col, live_count, lead, tile_cols, n_front, n_row, n_col):
    slots = contributions.shape[3]
    tile = contributions.shape[4]
    tiles = contributions.reshape(slots, tile, tile)
    fronts_to = target_front.reshape(slots)
    rows_to = target_row.reshape(slots)
    cols_to = target_col.reshape(slots)
    ids = jnp.arange(slots, dtype=jnp.int32)
    live = ids < live_count.reshape(())
    count = n_front * n_row
    capacity = max(2, -(-slots // count))
    me = lax.axis_index("front") * n_row + lax.axis_index("row")
    local_tile = rows_to // n_row * tile_cols + cols_to // n_col
    bucket_of = jnp.bitwise_xor(fronts_to * n_row + rows_to % n_row, me)
    earlier = (bucket_of[:, None] == bucket_of[None, :]) & live[None, :] & (ids[None, :] < ids[:, None])
    place = bucket_of * capacity + jnp.sum(earlier.astype(jnp.int32), axis=1)
    matches = (place[None, :] == jnp.arange(count * capacity, dtype=jnp.int32)[:, None]) & live[None, :]
    source = jnp.sum(jnp.where(matches, ids[None, :], 0), axis=1)
    filled = jnp.any(matches, axis=1)
    targets = jnp.sum(jnp.where(matches, local_tile[None, :], 0), axis=1)
    targets = jnp.where(filled, targets, -1).astype(BF16).reshape(count, 1, capacity)
    lines = jnp.pad(targets, ((0, 0), (0, 15), (0, tile - capacity)))
    segment = capacity * tile + 16
    packed = pl.pallas_call(
        functools.partial(pack_kernel, count, capacity),
        out_shape=tuple(jax.ShapeDtypeStruct((segment, tile), BF16) for _ in range(n_row))
        + (jax.ShapeDtypeStruct(((count - n_row) * segment, tile), BF16),),
        in_specs=[whole(pltpu.SMEM), whole(pl.ANY), whole(pl.ANY)],
        out_specs=tuple(whole(pl.ANY) for _ in range(n_row + 1)),
        scratch_shapes=[
            pltpu.VMEM((count * capacity, tile, tile), BF16),
            pltpu.SemaphoreType.DMA((count * capacity,)),
            pltpu.SemaphoreType.DMA((count * capacity,)),
            pltpu.SemaphoreType.DMA((count,)),
        ],
        compiler_params=pltpu.CompilerParams(vmem_limit_bytes=16 << 20),
        cost_estimate=estimate(5, 2 * slots * tile * tile * 2),
        name="pack",
    )(source, tiles, lines)
    near, far = packed[:n_row], packed[n_row]
    far = far.reshape(n_front - 1, n_row, segment, tile)
    others = [
        lax.ppermute(far[f - 1], "front", [(i, i ^ f) for i in range(n_front)])
        for f in range(1, n_front)
    ]
    groups = [jnp.concatenate([near[k]] + [other[k] for other in others]) for k in range(n_row)]
    groups, lead = lax.optimization_barrier((groups, lead))
    received = [groups[0]] + [
        lax.ppermute(groups[k], "row", [(i, i ^ k) for i in range(n_row)]) for k in range(1, n_row)
    ]
    arrived = jnp.stack(
        [group.reshape(n_front, segment, tile)[:, capacity * tile, :capacity] for group in received]
    )
    arrived = arrived.astype(jnp.int32).reshape(-1)
    return received, arrived, lead


def extend_kernel(groups, parts, capacity, tile_cols, first, arrived, front, *rest):
    received, out = rest[:groups], rest[groups]
    row = pl.program_id(0)
    tile = front.shape[2]
    last = first + out.shape[1]
    segment = capacity * tile + 16
    out[...] = front[:, first:last].astype(F32)
    for k in range(groups):
        for part in range(parts):
            for p in range(capacity):
                target = arrived[(k * parts + part) * capacity + p]
                column = target % tile_cols
                start = part * segment + p * tile

                @pl.when(
                    (target >= 0) & (target // tile_cols == row) & (column >= first) & (column < last)
                )
                def _():
                    out[0, column - first] += received[k][start : start + tile, :].astype(F32)


def extend(front, received, arrived, capacity, first, last, name):
    rows, tile_cols, tile, _ = front.shape
    cols = last - first
    count = len(received)
    parts = received[0].shape[0] // (capacity * tile + 16)
    return pl.pallas_call(
        functools.partial(extend_kernel, count, parts, capacity, tile_cols, first),
        out_shape=jax.ShapeDtypeStruct((rows, cols, tile, tile), F32),
        grid=(rows,),
        in_specs=[whole(pltpu.SMEM), pl.BlockSpec((1, last, tile, tile), lambda a: (a, 0, 0, 0))]
        + [whole()] * count,
        out_specs=pl.BlockSpec((1, cols, tile, tile), lambda a: (a, 0, 0, 0)),
        compiler_params=pltpu.CompilerParams(vmem_limit_bytes=48 << 20),
        cost_estimate=estimate(2 * cols, rows * last * tile * tile * 6),
        name=name,
    )(arrived, front, *received)


def solve_rows(coded, scales, index, t, high, low, tile):
    start = pl.multiple_of(t * tile, tile)
    parts = []
    for c in range(LEAD):
        k = jnp.bitwise_xor(index, c)
        values = coded[k, pl.ds(start, tile), :].astype(jnp.int32).astype(F32)
        parts.append(split(values * scales[k, t]))
    solved = []
    for n in range(LEAD):
        total = None
        for c in range(n + 1):
            rows = slice(n * tile, (n + 1) * tile)
            cols = slice(c * tile, (c + 1) * tile)
            term = mm3_nt(parts[c], (high[rows, cols], low[rows, cols]))
            total = term if total is None else total + term
        solved.append(total)
    return solved


def trailing_kernel(
    tile, n_row, n_col, tile_cols, row0, col0, spot, row_scales, col_scales, panel, work, by_row, by_col, high, low, own, out, cols_hi, cols_lo, rows_f
):
    a = pl.program_id(0)
    row_index, col_index = spot[0], spot[1]
    pieces = tile // LANES

    @pl.when(a == 0)
    def _():
        def body(b, carry):
            start = pl.multiple_of(b * tile, tile)
            solved = solve_rows(by_col, col_scales, row_index, b, high, low, tile)
            for n in range(LEAD):
                hi, lo = split(solved[n])
                cols_hi[pl.ds(start, tile), n * tile : (n + 1) * tile] = hi
                cols_lo[pl.ds(start, tile), n * tile : (n + 1) * tile] = lo
            return carry

        lax.fori_loop(0, tile_cols - col0, body, 0)

    global_row = a * n_row + row_index
    below = global_row >= LEAD

    def finish(b, value):
        for part in range(pieces):
            lanes = value[:, part * LANES : (part + 1) * LANES]
            out[pl.ds(b * pieces + part, tile, stride=tile_cols * pieces), :] = lanes

    @pl.when(below)
    def _():
        solved = solve_rows(by_row, row_scales, col_index, a - row0, high, low, tile)
        for n in range(LEAD):
            rows_f[n] = solved[n]
        rows = split(jnp.concatenate(solved, axis=1))
        for b in range(tile_cols):
            global_col = b * n_col + col_index
            if b * n_col < LEAD:

                @pl.when(global_col < LEAD)
                def _():
                    finish(b, rows_f[jnp.minimum(global_col, LEAD - 1)])

            if b * n_col + n_col > LEAD:

                @pl.when((global_col >= LEAD) & (global_col <= global_row))
                def _():
                    at = slice((b - col0) * tile, (b - col0 + 1) * tile)
                    update = mm3_nt(rows, (cols_hi[at, :], cols_lo[at, :]))
                    finish(b, (work[0, b - 1] if b else panel[0, 0]) - update)

                @pl.when((global_col >= LEAD) & (global_col > global_row))
                def _():
                    finish(b, jnp.zeros((tile, tile), F32))

    @pl.when(jnp.logical_not(below))
    def _():
        for b in range(tile_cols):
            finish(b, jnp.zeros((tile, tile), F32))

        @pl.when((col_index < LEAD) & (col_index <= row_index))
        def _():
            finish(0, own[...])


def trailing(panel, work, by_row, by_col, high, low, own, spot, tile, n_row, n_col, tile_rows, tile_cols, row0, col0):
    cols = tile_cols * tile
    width = LEAD * tile
    count = (tile_cols - col0) * tile
    lines = tile * cols // LANES
    return pl.pallas_call(
        functools.partial(trailing_kernel, tile, n_row, n_col, tile_cols, row0, col0),
        out_shape=jax.ShapeDtypeStruct((tile_rows * lines, LANES), F32),
        grid=(tile_rows,),
        in_specs=[whole(pltpu.SMEM)] * 3
        + [pl.BlockSpec((1, 1, tile, tile), lambda a: (a, 0, 0, 0))]
        + [pl.BlockSpec((1, tile_cols - 1, tile, tile), lambda a: (a, 0, 0, 0))]
        + [whole()] * 5,
        out_specs=pl.BlockSpec((lines, LANES), lambda a: (a, 0)),
        scratch_shapes=[
            pltpu.VMEM((count, width), BF16),
            pltpu.VMEM((count, width), BF16),
            pltpu.VMEM((LEAD, tile, tile), F32),
        ],
        compiler_params=pltpu.CompilerParams(vmem_limit_bytes=56 << 20),
        cost_estimate=estimate(25, tile_rows * lines * LANES * 8),
        name="trailing",
    )(spot, decode_scales(by_row, tile), decode_scales(by_col, tile), panel, work, by_row, by_col, high, low, own)


def encode(piece, tile):
    tiles = piece.reshape(-1, tile, tile)
    largest = jnp.max(jnp.abs(tiles), axis=(1, 2))
    power = jnp.floor(jnp.log2(jnp.maximum(largest, 1e-30))) + 1.0
    half = jnp.floor(0.5 * power)
    shrunk = tiles * jnp.exp2(-half)[:, None, None]
    codes = jnp.round(shrunk * (jnp.exp2(half - power) * TOP)[:, None, None]).astype(jnp.int16)
    line = jnp.zeros((16, tile), jnp.int16).at[0, : tiles.shape[0]].set(power.astype(jnp.int16))
    return jnp.concatenate([codes.reshape(-1, tile), line], axis=0)


def decode_scales(coded, tile):
    rows = coded.shape[1] - 16
    return jnp.exp2(coded[:, rows, : rows // tile].astype(F32) - 14.0) * (16384.0 / TOP)


def partner(piece, axis, size, k):
    return lax.ppermute(piece, axis, [(i, i ^ k) for i in range(size)])


def exchange(piece, axis, size, first=1):
    return [partner(piece, axis, size, k) for k in range(first, size)]


def per_device(front_matrix, contributions, target_front, target_row, target_col, live_count):
    tile_rows = front_matrix.shape[1]
    tile = front_matrix.shape[3]
    tile_cols = front_matrix.shape[4]
    n_front = lax.axis_size("front")
    n_row = lax.axis_size("row")
    n_col = lax.axis_size("col")
    spot = jnp.stack([lax.axis_index("row"), lax.axis_index("col")]).astype(jnp.int32)
    row0, col0 = LEAD // n_row, LEAD // n_col

    line = front_matrix[0, 0, 0, :, 0, 0, :]
    line = jnp.stack([line] + exchange(line, "col", n_col))
    lead = [line] + exchange(line, "row", n_row)
    front = front_matrix.reshape(tile_rows, tile, tile_cols, tile).transpose(0, 2, 1, 3)
    capacity = max(2, -(-contributions.shape[3] // (n_front * n_row)))
    received, arrived, lead = route_tiles(
        contributions, target_front, target_row, target_col, live_count, lead, tile_cols, n_front, n_row, n_col
    )
    lower0, inverse0 = lead_first(lead, spot, tile)
    arrived, lower0 = lax.optimization_barrier((arrived, lower0))
    panel = extend(front, received, arrived, capacity, 0, 1, "extend_panel")
    coded = encode(panel[row0:, 0].reshape(-1, tile), tile)
    coded, inverse0 = lax.optimization_barrier((coded, inverse0))
    mirrored = lax.ppermute(
        coded,
        ("row", "col"),
        [(r * n_col + c, c * n_col + r) for r in range(n_row) for c in range(n_col)],
    )
    left, work1, lower1, inverse1 = lead_second(lead, inverse0, spot, tile)
    beside = partner(coded, "col", n_col, 1)
    mirrored, coded, work1, arrived = lax.optimization_barrier((mirrored, coded, work1, arrived))
    by_row = [coded, beside] + exchange(coded, "col", n_col, 2)
    by_col = [mirrored] + exchange(mirrored, "row", n_row)
    work = extend(front, received, arrived, capacity, 1, tile_cols, "extend_rest")
    high, low, own = lead_third(lower0, inverse0, left, work1, lower1, inverse1, spot, tile)
    factor = trailing(
        panel,
        work,
        jnp.stack(by_row),
        jnp.stack(by_col),
        high,
        low,
        own,
        spot,
        tile,
        n_row,
        n_col,
        tile_rows,
        tile_cols,
        row0,
        col0,
    )
    return factor.reshape(1, tile_rows, 1, tile, tile_cols, 1, tile)


def solution(mesh):
    in_specs = (
        P("front", None, "row", None, None, "col", None),
        P("front", "row", "col", None, None, None),
        P("front", "row", "col", None),
        P("front", "row", "col", None),
        P("front", "row", "col", None),
        P("front", "row", "col"),
    )
    out_specs = P("front", None, "row", None, None, "col", None)
    return jax.shard_map(
        per_device, mesh=mesh, in_specs=in_specs, out_specs=out_specs, check_vma=False
    )
```
